256 devices in a mesh: branch: 2 (over z_lo), seq: 8 (over x, core), dp: 16 (over y, z_hi).
Axes of the slice: x: 4, y: 4, z: 8 (z_hi: 4, z_lo: 2; z = z_hi * 2 + z_lo), core: 2. Of those that a mesh axis runs over, the one named last changes fastest.
Arguments:
- queries: bfloat16 [2, 16, 1024, 3072], P('branch', 'dp', 'seq'), may hold values from -8 to 8
- keys: bfloat16 [2, 16, 1024, 3072], P('branch', 'dp', 'seq'), may hold values from -8 to 8
- values: bfloat16 [2, 16, 1024, 3072], P('branch', 'dp', 'seq'), may hold values from -6 to 6
- cotangent: bfloat16 [2, 16, 1024, 5120], P('branch', 'dp', 'seq'), may hold values from -3 to 3
- gate: float32 [2, 16, 5120], P('branch', 'dp'), may hold values from 0.1 to 1.9
- w_out: bfloat16 [2, 3072, 5120], P('branch', ('seq', 'dp')), may hold values from -0.109375 to 0.109375
Outputs:
- grad_queries: bfloat16 [2, 16, 1024, 3072], P('branch', 'dp', 'seq')
- grad_keys: bfloat16 [2, 16, 1024, 3072], P('branch', 'dp', 'seq')
- grad_values: bfloat16 [2, 16, 1024, 3072], P('branch', 'dp', 'seq')
- grad_weight: float32 [2, 3072, 5120], P('branch', ('seq', 'dp'))
The draws below stay inside these ranges and needn't reach their ends.
All inputs are finite; a program needn't handle non-finite values.
Results may differ from the reference program's by a relative error of at most 0.0088.
Values may be sent and summed in bfloat16 or wider, within the bound.
No kernel may reach another device: no remote copies, remote signals or barrier semaphores. Data moves between devices by JAX's collectives and lax.ppermute only.
A program may use at most 128 MiB of HBM per device.

```python
import jax
import jax.numpy as jnp
from jax import lax

D = 5120
H = 24
HD = 128
SEQLEN = 1024
CLIPS = 16


def draw_queries(key, part):
    key = jax.random.fold_in(key, 1)
    result = 1.2 * jax.random.truncated_normal(key, -6.0, 6.0, (2, CLIPS, SEQLEN, H * HD), jnp.float32)
    return result.astype(jnp.bfloat16)


def draw_keys(key, part):
    key = jax.random.fold_in(key, 2)
    result = 1.2 * jax.random.truncated_normal(key, -6.0, 6.0, (2, CLIPS, SEQLEN, H * HD), jnp.float32)
    return result.astype(jnp.bfloat16)


def block_levels(rng, shape, shards, low, high):
    def one(axis_at, parts):
        heights = jax.random.uniform(jax.random.fold_in(jax.random.fold_in(rng, 6), axis_at), (parts,), jnp.float32, low / len(shards), high / len(shards))
        return jnp.repeat(jnp.exp(heights), shape[axis_at] // parts).reshape((-1,) + (1,) * (len(shape) - axis_at - 1))

    gain = one(*shards[0])
    for cut in shards[1:]:
        gain = gain * one(*cut)
    return gain


def bell_draw(rng, extent, deviation, most, pieces=(), dtype=jnp.bfloat16):
    values = deviation * jax.random.normal(rng, extent, jnp.float32)
    if pieces:
        values = values * block_levels(rng, extent, pieces, -0.22, 0.18)
    return jnp.clip(values, -most, most).astype(dtype)


def setup_inputs(seed: int = 0) -> dict:
    streams_of = jax.random.split(jax.random.key(seed), 7)
    return {
        "queries": draw_queries(jax.random.fold_in(streams_of[6], 71), 0),
        "keys": draw_keys(jax.random.fold_in(streams_of[6], 71), 0),
        "values": bell_draw(streams_of[2], (2, CLIPS, SEQLEN, H * HD), 1.0, 6.0, ((0, 2), (1, 16), (2, 8))),
        "cotangent": bell_draw(streams_of[3], (2, CLIPS, SEQLEN, D), 0.5, 3.0, ((0, 2), (1, 16), (2, 8))),
        "gate": jnp.clip(1.0 + 0.18 * jax.random.normal(streams_of[4], (2, CLIPS, D), jnp.float32), 0.1, 1.9),
        "w_out": bell_draw(streams_of[5], (2, H * HD, D), (H * HD) ** -0.5, 0.109375, ((0, 2), (1, 128))),
    }


def head_pass(head_query, head_key, head_value, head_grad):
    score_scale = HD ** -0.5
    scores = jnp.dot(head_query, head_key.T, preferred_element_type=jnp.float32) * score_scale
    row_max = jnp.max(scores, axis=-1, keepdims=True)
    exponent = jnp.exp(scores - row_max)
    softmax_rows = exponent / jnp.sum(exponent, axis=-1, keepdims=True)
    rounded = softmax_rows.astype(jnp.bfloat16)
    attended = jnp.dot(rounded, head_value, preferred_element_type=jnp.float32).astype(jnp.bfloat16)
    grad_values = jnp.dot(rounded.T, head_grad, preferred_element_type=jnp.float32).astype(jnp.bfloat16)
    grad_probs = jnp.dot(head_grad, head_value.T, preferred_element_type=jnp.float32)
    row_delta = jnp.sum(head_grad.astype(jnp.float32) * attended.astype(jnp.float32), axis=-1, keepdims=True)
    grad_scores = (softmax_rows * (grad_probs - row_delta) * score_scale).astype(jnp.bfloat16)
    grad_queries = jnp.dot(grad_scores, head_key, preferred_element_type=jnp.float32).astype(jnp.bfloat16)
    grad_keys = jnp.dot(grad_scores.T, head_query, preferred_element_type=jnp.float32).astype(jnp.bfloat16)
    return attended, grad_queries, grad_keys, grad_values


def split_heads(array):
    return array.reshape(SEQLEN, H, HD).transpose(1, 0, 2)


def merge_heads(array):
    return array.transpose(1, 0, 2).reshape(SEQLEN, H * HD)


def one_head(members):
    return head_pass(members[0], members[1], members[2], members[3])


def reference(queries, keys, values, cotangent, gate, w_out):
    query_list = []
    key_list = []
    value_list = []
    weight_list = []
    for branch in range(2):
        combined = cotangent[branch].astype(jnp.float32)
        if branch == 1:
            combined = combined + cotangent[0].astype(jnp.float32)
        grad_out = (gate[branch][:, None, :] * combined).astype(jnp.bfloat16)
        weights = w_out[branch]

        def clip_pass(running, inputs):
            clip_query, clip_key, clip_value, clip_grad = inputs
            grad_heads = jnp.dot(clip_grad, weights.T, preferred_element_type=jnp.float32).astype(jnp.bfloat16)
            attended, grad_q, grad_k, grad_v = lax.map(one_head, (split_heads(clip_query), split_heads(clip_key), split_heads(clip_value), split_heads(grad_heads)))
            running = running + jnp.dot(merge_heads(attended).T, clip_grad, preferred_element_type=jnp.float32)
            return running, (merge_heads(grad_q), merge_heads(grad_k), merge_heads(grad_v))

        start_value = jnp.zeros((H * HD, D), jnp.float32)
        summed, grads = lax.scan(clip_pass, start_value, (queries[branch], keys[branch], values[branch], grad_out))
        query_list.append(grads[0])
        key_list.append(grads[1])
        value_list.append(grads[2])
        weight_list.append(summed)
    return (jnp.stack(query_list), jnp.stack(key_list), jnp.stack(value_list), jnp.stack(weight_list))
```

```python
import functools

import jax
import jax.numpy as jnp
from jax import lax
from jax.experimental import pallas as pl
from jax.experimental.pallas import tpu as pltpu
from jax.sharding import Mesh, PartitionSpec as P

HD = 128
XS, CS, YS, ZS = 4, 2, 4, 4
RANKS = XS * CS
TOK = 128
SEQ = RANKS * TOK
NH = 3
WIDTH = NH * HD
D = 5120
QB = 256
TILE = 512
SCALE = HD**-0.5
LOG2E = 1.4426950408889634
F32 = jnp.float32
BF16 = jnp.bfloat16
NT = (((1,), (1,)), ((), ()))
NN = (((1,), (0,)), ((), ()))
VMEM_LIMIT = 56 * 1024 * 1024


def dot(a, b, dims=NN):
    return lax.dot_general(a, b, dims, preferred_element_type=F32)


def params(**more):
    return pltpu.CompilerParams(vmem_limit_bytes=VMEM_LIMIT, **more)


def cost(flops, nbytes, trans=0):
    return pl.CostEstimate(flops=flops, bytes_accessed=nbytes, transcendentals=trans)


def pack_body(q_ref, k_ref, v_ref, out_ref):
    out_ref[0, 0] = q_ref[...]
    out_ref[0, 1] = k_ref[...]
    out_ref[0, 2] = v_ref[...]


def pack(q, k, v):
    spec = pl.BlockSpec((TOK, WIDTH), lambda j: (0, j))
    return pl.pallas_call(
        pack_body,
        grid=(RANKS,),
        in_specs=[spec] * 3,
        out_specs=pl.BlockSpec((1, 3, TOK, WIDTH), lambda j: (j, 0, 0, 0)),
        out_shape=jax.ShapeDtypeStruct((RANKS, 3, TOK, WIDTH), BF16),
        compiler_params=params(),
        cost_estimate=cost(0, 2 * 3 * 2 * SEQ * WIDTH),
        name="pack",
    )(q, k, v)


def unpack_body(a_ref, b_ref, q_ref, k_ref, v_ref):
    split = a_ref.shape[-1]
    for i, ref in enumerate((q_ref, k_ref, v_ref)):
        ref[:, :split] = a_ref[0, i]
        ref[:, split:] = b_ref[0, i]


def unpack(a, b):
    def spec(array):
        return pl.BlockSpec((1, 3, TOK, array.shape[-1]), lambda j: (j, 0, 0, 0))

    out = pl.BlockSpec((TOK, WIDTH), lambda j: (0, j))
    return pl.pallas_call(
        unpack_body,
        grid=(RANKS,),
        in_specs=[spec(a), spec(b)],
        out_specs=[out] * 3,
        out_shape=[jax.ShapeDtypeStruct((TOK, RANKS * WIDTH), BF16)] * 3,
        compiler_params=params(),
        cost_estimate=cost(0, 2 * 3 * 2 * SEQ * WIDTH),
        name="unpack",
    )(a, b)


def forward_body(slot_ref, qkv_ref, prob_ref, att_ref, q_s, k_s, vt_s):
    block = pl.program_id(1)

    @pl.when(block == 0)
    def _():
        for s in range(RANKS):
            rows = pl.ds(s * TOK, TOK)
            piece = slot_ref[s]
            q_s[rows, :] = qkv_ref[piece, 0]
            k_s[rows, :] = qkv_ref[piece, 1]
            vt_s[:, rows] = qkv_ref[piece, 2].astype(F32).T.astype(BF16)

    q = q_s[pl.ds(pl.multiple_of(block * QB, QB), QB), :]
    scores = dot(k_s[...], q, NT)
    top = jnp.max(scores, axis=0, keepdims=True)
    e = jnp.exp2((scores - top) * (SCALE * LOG2E))
    norm = 1.0 / jnp.sum(e, axis=0, keepdims=True)
    prob = (e * norm).astype(BF16)
    prob_ref[0] = prob
    att_ref[...] = dot(vt_s[...], prob).astype(BF16)


def forward(slots, qkv):
    return pl.pallas_call(
        forward_body,
        grid_spec=pltpu.PrefetchScalarGridSpec(
            num_scalar_prefetch=1,
            grid=(NH, SEQ // QB),
            in_specs=[pl.BlockSpec((RANKS, 3, TOK, HD), lambda h, b, s: (0, 0, 0, h))],
            out_specs=[
                pl.BlockSpec((1, SEQ, QB), lambda h, b, s: (h, 0, b)),
                pl.BlockSpec((HD, QB), lambda h, b, s: (h, b)),
            ],
            scratch_shapes=[
                pltpu.VMEM((SEQ, HD), BF16),
                pltpu.VMEM((SEQ, HD), BF16),
                pltpu.VMEM((HD, SEQ), BF16),
            ],
        ),
        out_shape=[
            jax.ShapeDtypeStruct((NH, SEQ, SEQ), BF16),
            jax.ShapeDtypeStruct((WIDTH, SEQ), BF16),
        ],
        compiler_params=params(),
        cost_estimate=cost(4 * NH * SEQ * SEQ * HD, 2 * NH * SEQ * SEQ + 8 * SEQ * WIDTH, NH * SEQ * SEQ),
        name="forward",
    )(slots, qkv)


def backward_body(slot_ref, qkv_ref, prob_ref, gt_ref, att_ref, out_ref, q_s, v_s, kt_s, dk_s, dv_s):
    block = pl.program_id(1)
    last = pl.num_programs(1) - 1

    @pl.when(block == 0)
    def _():
        for s in range(RANKS):
            rows = pl.ds(s * TOK, TOK)
            piece = slot_ref[s]
            q_s[rows, :] = qkv_ref[piece, 0]
            kt_s[:, rows] = qkv_ref[piece, 1].astype(F32).T.astype(BF16)
            v_s[rows, :] = qkv_ref[piece, 2]
        dk_s[...] = jnp.zeros_like(dk_s)
        dv_s[...] = jnp.zeros_like(dv_s)

    gt = gt_ref[...]
    prob = prob_ref[0]
    delta = jnp.sum(gt.astype(F32) * att_ref[...].astype(F32), axis=0, keepdims=True)
    dprob = dot(v_s[...], gt)
    dscore = (prob.astype(F32) * ((dprob - delta) * SCALE)).astype(BF16)
    q = q_s[pl.ds(pl.multiple_of(block * QB, QB), QB), :]
    dv_s[...] += dot(prob, gt, NT)
    dk_s[...] += dot(dscore, q)
    dq = dot(kt_s[...], dscore).T.astype(BF16)
    for i in range(QB // TOK):
        out_ref[slot_ref[block * (QB // TOK) + i], 0] = dq[i * TOK : (i + 1) * TOK]

    @pl.when(block == last)
    def _():
        for s in range(RANKS):
            rows = pl.ds(s * TOK, TOK)
            out_ref[slot_ref[s], 1] = dk_s[rows, :].astype(BF16)
            out_ref[slot_ref[s], 2] = dv_s[rows, :].astype(BF16)


def backward(slots, qkv, prob, gt, att, first, count):
    return pl.pallas_call(
        backward_body,
        grid_spec=pltpu.PrefetchScalarGridSpec(
            num_scalar_prefetch=1,
            grid=(count, SEQ // QB),
            in_specs=[
                pl.BlockSpec((RANKS, 3, TOK, HD), lambda h, b, s: (0, 0, 0, h + first)),
                pl.BlockSpec((1, SEQ, QB), lambda h, b, s: (h + first, 0, b)),
                pl.BlockSpec((HD, QB), lambda h, b, s: (h + first, b)),
                pl.BlockSpec((HD, QB), lambda h, b, s: (h + first, b)),
            ],
            out_specs=pl.BlockSpec((RANKS, 3, TOK, HD), lambda h, b, s: (0, 0, 0, h)),
            scratch_shapes=[
                pltpu.VMEM((SEQ, HD), BF16),
                pltpu.VMEM((SEQ, HD), BF16),
                pltpu.VMEM((HD, SEQ), BF16),
                pltpu.VMEM((SEQ, HD), F32),
                pltpu.VMEM((SEQ, HD), F32),
            ],
        ),
        out_shape=jax.ShapeDtypeStruct((RANKS, 3, TOK, count * HD), BF16),
        compiler_params=params(),
        cost_estimate=cost(8 * count * SEQ * SEQ * HD, 2 * count * SEQ * (SEQ + 8 * HD), 0),
        name="backward",
    )(slots, qkv, prob, gt, att)


def weight_body(att_ref, *refs):
    out_ref = refs[-1]
    rows = jnp.concatenate([ref[...] for ref in refs[:-1]], axis=0)
    out_ref[...] = dot(att_ref[...], rows).astype(BF16)


def weight_grad(att, pieces):
    wide = pieces[0].shape[1]
    piece = pl.BlockSpec((TOK, TILE), lambda j: (0, j))
    return pl.pallas_call(
        weight_body,
        grid=(wide // TILE,),
        in_specs=[pl.BlockSpec((WIDTH, SEQ), lambda j: (0, 0))] + [piece] * RANKS,
        out_specs=pl.BlockSpec((WIDTH, TILE), lambda j: (0, j)),
        out_shape=jax.ShapeDtypeStruct((WIDTH, wide), BF16),
        compiler_params=params(),
        cost_estimate=cost(2 * WIDTH * SEQ * wide, 2 * (WIDTH * SEQ + SEQ * wide + WIDTH * wide)),
        name="weight_grad",
    )(att, *pieces)


def heads_body(count, carry, w_ref, *refs):
    acc_ref = refs[-1]
    out_ref = refs[-2]
    step = pl.program_id(0)

    @pl.when(step == 0)
    def _():
        acc_ref[...] = refs[RANKS][...] if carry else jnp.zeros_like(acc_ref)

    rows = jnp.concatenate([ref[...] for ref in refs[:RANKS]], axis=0)
    acc_ref[...] += dot(w_ref[...], rows, NT)

    @pl.when(step == count - 1)
    def _():
        out_ref[...] = acc_ref[...].astype(out_ref.dtype)


def heads_grad(weights, offset, pieces, carry, dtype):
    wide = pieces[0].shape[1]
    count = wide // TILE
    first = offset // TILE
    piece = pl.BlockSpec((TOK, TILE), lambda j: (0, j))
    whole = pl.BlockSpec((WIDTH, SEQ), lambda j: (0, 0))
    extra = [] if carry is None else [carry]
    return pl.pallas_call(
        functools.partial(heads_body, count, carry is not None),
        grid=(count,),
        in_specs=[pl.BlockSpec((WIDTH, TILE), lambda j: (0, j + first))]
        + [piece] * RANKS
        + [whole] * len(extra),
        out_specs=whole,
        out_shape=jax.ShapeDtypeStruct((WIDTH, SEQ), dtype),
        scratch_shapes=[pltpu.VMEM((WIDTH, SEQ), F32)],
        compiler_params=params(),
        cost_estimate=cost(2 * WIDTH * SEQ * wide, 2 * (WIDTH * SEQ + SEQ * wide + WIDTH * wide)),
        name="heads_grad",
    )(weights, *pieces, *extra)


def rank(x, c):
    return (x % XS) * CS + c


ONWARD = [(rank(x, c), rank(x + 1 - 2 * c, c)) for x in range(XS) for c in range(CS)]
SIBLING = [(rank(x, c), rank(x, 1 - c)) for x in range(XS) for c in range(CS)]


def gather_rows(own):
    seq = ("x", "c")
    send = lambda value, perm: lax.ppermute(value, seq, perm)
    near = send(own, ONWARD)
    sib = send(own, SIBLING)
    near_sib = send(sib, ONWARD)
    far = send(near, ONWARD)
    back = send(near, SIBLING)
    back_sib = send(near_sib, SIBLING)
    far_sib = send(far, SIBLING)
    return [own, sib, near, near_sib, back, back_sib, far, far_sib]


def slot_table():
    x, c = lax.axis_index("x"), lax.axis_index("c")
    step = 1 - 2 * c
    at = lambda xx, cc: lax.rem(xx + 2 * XS, XS) * CS + cc
    return jnp.stack(
        [
            at(x, c),
            at(x, 1 - c),
            at(x - step, c),
            at(x - step, 1 - c),
            at(x + step, 1 - c),
            at(x + step, c),
            at(x + 2, c),
            at(x + 2, 1 - c),
        ]
    ).astype(jnp.int32)


def exchange(value, axis):
    return lax.all_to_all(value, axis, split_axis=0, concat_axis=0, tiled=True)


def scatter_sum(term):
    wide = term.shape[1]
    got = exchange(term.reshape(YS, WIDTH // YS, wide), "y")
    part = jnp.sum(got.astype(F32), axis=0).astype(BF16)
    got = exchange(part.reshape(ZS, WIDTH // (YS * ZS), wide), "z")
    return jnp.sum(got.astype(F32), axis=0)


def local(queries, keys, values, cotangent, gate, w_out):
    slots = slot_table()
    cot = cotangent[0, 0]
    chunks = (2560, 2560)
    starts = (0, 2560)

    weights = lax.all_gather(w_out[0], ("y", "z"), axis=0, tiled=True)
    qkv = exchange(pack(queries[0, 0], keys[0, 0], values[0, 0]), ("x", "c"))
    pieces = []
    for start, wide in zip(starts, chunks):
        mine = cot[:, start : start + wide]
        other = lax.ppermute(mine, "b", [(0, 1)])
        total = mine.astype(F32) + other.astype(F32)
        grad_out = (gate[0, :, start : start + wide] * total).astype(BF16)
        pieces.append(gather_rows(grad_out))
    prob, att = forward(slots, qkv)
    grad_weight = [scatter_sum(weight_grad(att, p)) for p in pieces]
    acc = heads_grad(weights, starts[0], pieces[0], None, F32)
    gt = heads_grad(weights, starts[1], pieces[1], acc, BF16)
    home = [
        exchange(backward(slots, qkv, prob, gt, att, first, count), ("x", "c"))
        for first, count in ((0, 1), (1, 2))
    ]
    dq, dk, dv = unpack(*home)
    return (
        dq[None, None],
        dk[None, None],
        dv[None, None],
        jnp.concatenate(grad_weight, axis=1)[None],
    )


def solution(mesh):
    fine = Mesh(mesh.devices.reshape(2, XS, CS, YS, ZS), ("b", "x", "c", "y", "z"))
    tokens = P("b", ("y", "z"), ("x", "c"), None)
    weight = P("b", ("x", "c", "y", "z"), None)
    return jax.shard_map(
        local,
        mesh=fine,
        in_specs=(tokens, tokens, tokens, tokens, P("b", ("y", "z"), None), weight),
        out_specs=(tokens, tokens, tokens, weight),
        check_vma=False,
    )
```

```python
import functools

import jax
import jax.numpy as jnp
from jax import lax
from jax.experimental import pallas as pl
from jax.experimental.pallas import tpu as pltpu
from jax.sharding import Mesh, PartitionSpec as P

HD = 128
XS, CS, YS, ZS = 4, 2, 4, 4
RANKS = XS * CS
TOK = 128
SEQ = RANKS * TOK
NH = 3
WIDTH = NH * HD
D = 5120
QB = 256
TILE = 512
SCALE = HD**-0.5
LOG2E = 1.4426950408889634
F32 = jnp.float32
BF16 = jnp.bfloat16
NT = (((1,), (1,)), ((), ()))
NN = (((1,), (0,)), ((), ()))
CHUNKS = (2560, 2560)
STARTS = tuple(sum(CHUNKS[:i]) for i in range(len(CHUNKS)))
GROUPS = ((0, 1), (1, 2))
VMEM_LIMIT = 56 * 1024 * 1024


def dot(a, b, dims=NN):
    return lax.dot_general(a, b, dims, preferred_element_type=F32)


def params(**more):
    return pltpu.CompilerParams(vmem_limit_bytes=VMEM_LIMIT, **more)


def cost(flops, nbytes, trans=0):
    return pl.CostEstimate(flops=flops, bytes_accessed=nbytes, transcendentals=trans)


def hbm(count):
    return [pl.BlockSpec(memory_space=pl.ANY)] * count


def pack_body(col_ref, q_ref, k_ref, v_ref, *out_refs):
    for s, out in enumerate(out_refs):
        cols = pl.ds(pl.multiple_of(col_ref[s] * WIDTH, WIDTH), WIDTH)
        for i, ref in enumerate((q_ref, k_ref, v_ref)):
            out[i] = ref[:, cols]


def pack(targets, q, k, v):
    whole = pl.BlockSpec((TOK, RANKS * WIDTH), lambda j, s: (0, 0))
    return pl.pallas_call(
        pack_body,
        grid_spec=pltpu.PrefetchScalarGridSpec(
            num_scalar_prefetch=1,
            grid=(1,),
            in_specs=[whole] * 3,
            out_specs=[pl.BlockSpec((3, TOK, WIDTH), lambda j, s: (0, 0, 0))] * RANKS,
        ),
        out_shape=[jax.ShapeDtypeStruct((3, TOK, WIDTH), BF16)] * RANKS,
        compiler_params=params(),
        cost_estimate=cost(0, 2 * 3 * 2 * SEQ * WIDTH),
        name="pack",
    )(targets, q, k, v)


def unpack_body(widths, col_ref, *refs):
    outs = refs[-3:]
    for s in range(RANKS):
        base = pl.multiple_of(col_ref[s] * WIDTH, WIDTH)
        at = 0
        for g, wide in enumerate(widths):
            cols = pl.ds(pl.multiple_of(base + at, HD), wide)
            for i, out in enumerate(outs):
                out[:, cols] = refs[g * RANKS + s][i]
            at += wide


def unpack(targets, groups):
    widths = tuple(g[0].shape[-1] for g in groups)
    pieces = [p for g in groups for p in g]
    whole = pl.BlockSpec((TOK, RANKS * WIDTH), lambda j, s: (0, 0))
    return pl.pallas_call(
        functools.partial(unpack_body, widths),
        grid_spec=pltpu.PrefetchScalarGridSpec(
            num_scalar_prefetch=1,
            grid=(1,),
            in_specs=[pl.BlockSpec(p.shape, lambda j, s: (0, 0, 0)) for p in pieces],
            out_specs=[whole] * 3,
        ),
        out_shape=[jax.ShapeDtypeStruct((TOK, RANKS * WIDTH), BF16)] * 3,
        compiler_params=params(),
        cost_estimate=cost(0, 2 * 3 * 2 * SEQ * WIDTH),
        name="unpack",
    )(targets, *pieces)


def gate_body(gate_ref, mine_ref, other_ref, out_ref):
    total = mine_ref[...].astype(F32) + other_ref[...].astype(F32)
    out_ref[...] = (gate_ref[...] * total).astype(BF16)


def gated(gate, cot, other, start):
    wide = other.shape[1]
    at = start // TILE
    return pl.pallas_call(
        gate_body,
        grid=(wide // TILE,),
        in_specs=[
            pl.BlockSpec((1, TILE), lambda j: (0, j + at)),
            pl.BlockSpec((TOK, TILE), lambda j: (0, j + at)),
            pl.BlockSpec((TOK, TILE), lambda j: (0, j)),
        ],
        out_specs=pl.BlockSpec((TOK, TILE), lambda j: (0, j)),
        out_shape=jax.ShapeDtypeStruct((TOK, wide), BF16),
        compiler_params=params(),
        cost_estimate=cost(2 * TOK * wide, 6 * TOK * wide),
        name="gated",
    )(gate, cot, other)


def forward_body(*refs):
    pieces = refs[:RANKS]
    prob_ref, att_ref, q_s, k_s, vt_s = refs[-5:]
    block = pl.program_id(1)

    @pl.when(block == 0)
    def _():
        for s, piece in enumerate(pieces):
            rows = pl.ds(s * TOK, TOK)
            q_s[rows, :] = piece[0]
            k_s[rows, :] = piece[1]
            vt_s[:, rows] = piece[2].astype(F32).T.astype(BF16)

    q = q_s[pl.ds(pl.multiple_of(block * QB, QB), QB), :]
    scores = dot(k_s[...], q, NT)
    top = jnp.max(scores, axis=0, keepdims=True)
    e = jnp.exp2((scores - top) * (SCALE * LOG2E))
    norm = 1.0 / jnp.sum(e, axis=0, keepdims=True)
    prob = (e * norm).astype(BF16)
    prob_ref[0] = prob
    att_ref[...] = dot(vt_s[...], prob).astype(BF16)


def forward(qkv, after=()):
    return pl.pallas_call(
        forward_body,
        grid=(NH, SEQ // QB),
        in_specs=[pl.BlockSpec((3, TOK, HD), lambda h, b: (0, 0, h))] * RANKS + hbm(len(after)),
        out_specs=[
            pl.BlockSpec((1, SEQ, QB), lambda h, b: (h, 0, b)),
            pl.BlockSpec((HD, QB), lambda h, b: (h, b)),
        ],
        scratch_shapes=[
            pltpu.VMEM((SEQ, HD), BF16),
            pltpu.VMEM((SEQ, HD), BF16),
            pltpu.VMEM((HD, SEQ), BF16),
        ],
        out_shape=[
            jax.ShapeDtypeStruct((NH, SEQ, SEQ), BF16),
            jax.ShapeDtypeStruct((WIDTH, SEQ), BF16),
        ],
        compiler_params=params(),
        cost_estimate=cost(4 * NH * SEQ * SEQ * HD, 2 * NH * SEQ * SEQ + 8 * SEQ * WIDTH, NH * SEQ * SEQ),
        name="forward",
    )(*qkv, *after)


def backward_body(*refs):
    pieces = refs[:RANKS]
    prob_ref, gt_ref, att_ref = refs[RANKS : RANKS + 3]
    outs = refs[-5 - RANKS : -5]
    q_s, v_s, kt_s, dk_s, dv_s = refs[-5:]
    block = pl.program_id(1)
    last = pl.num_programs(1) - 1

    @pl.when(block == 0)
    def _():
        for s, piece in enumerate(pieces):
            rows = pl.ds(s * TOK, TOK)
            q_s[rows, :] = piece[0]
            kt_s[:, rows] = piece[1].astype(F32).T.astype(BF16)
            v_s[rows, :] = piece[2]
        dk_s[...] = jnp.zeros_like(dk_s)
        dv_s[...] = jnp.zeros_like(dv_s)

    gt = gt_ref[...]
    prob = prob_ref[0]
    delta = jnp.sum(gt.astype(F32) * att_ref[...].astype(F32), axis=0, keepdims=True)
    dprob = dot(v_s[...], gt)
    dscore = (prob.astype(F32) * ((dprob - delta) * SCALE)).astype(BF16)
    q = q_s[pl.ds(pl.multiple_of(block * QB, QB), QB), :]
    dv_s[...] += dot(prob, gt, NT)
    dk_s[...] += dot(dscore, q)
    dq = dot(kt_s[...], dscore).T.astype(BF16)
    for s, out in enumerate(outs):
        i = s % (QB // TOK)

        @pl.when(block == s // (QB // TOK))
        def _():
            out[0] = dq[i * TOK : (i + 1) * TOK]

    @pl.when(block == last)
    def _():
        for s, out in enumerate(outs):
            rows = pl.ds(s * TOK, TOK)
            out[1] = dk_s[rows, :].astype(BF16)
            out[2] = dv_s[rows, :].astype(BF16)


def backward(qkv, prob, gt, att, first, count, after=()):
    return pl.pallas_call(
        backward_body,
        grid=(count, SEQ // QB),
        in_specs=[pl.BlockSpec((3, TOK, HD), lambda h, b: (0, 0, h + first))] * RANKS
        + [
            pl.BlockSpec((1, SEQ, QB), lambda h, b: (h + first, 0, b)),
            pl.BlockSpec((HD, QB), lambda h, b: (h + first, b)),
            pl.BlockSpec((HD, QB), lambda h, b: (h + first, b)),
        ]
        + hbm(len(after)),
        out_specs=[pl.BlockSpec((3, TOK, HD), lambda h, b: (0, 0, h))] * RANKS,
        scratch_shapes=[
            pltpu.VMEM((SEQ, HD), BF16),
            pltpu.VMEM((SEQ, HD), BF16),
            pltpu.VMEM((HD, SEQ), BF16),
            pltpu.VMEM((SEQ, HD), F32),
            pltpu.VMEM((SEQ, HD), F32),
        ],
        out_shape=[jax.ShapeDtypeStruct((3, TOK, count * HD), BF16)] * RANKS,
        compiler_params=params(),
        cost_estimate=cost(8 * count * SEQ * SEQ * HD, 2 * count * SEQ * (SEQ + 8 * HD), 0),
        name="backward",
    )(*qkv, prob, gt, att, *after)


def weight_body(count, at_ref, att_ref, *refs):
    outs, wide_s, att_s = refs[-2 - YS : -2], refs[-2], refs[-1]
    block, row = WIDTH // YS, WIDTH // (YS * ZS)

    @pl.when(pl.program_id(0) == 0)
    def _():
        wide_s[...] = att_ref[...].astype(F32)
        for i in range(YS * ZS):
            start = pl.multiple_of(at_ref[i] * row, 8)
            att_s[pl.ds(i * row, row), :] = wide_s[pl.ds(start, row), :]

    rows = jnp.concatenate([ref[...] for ref in refs[:RANKS]], axis=0)
    term = dot(att_s[...].astype(BF16), rows).astype(BF16)
    for i, out in enumerate(outs):
        out[...] = term[i * block : (i + 1) * block]


def weight_grad(order, att, pieces, after=()):
    wide = pieces[0].shape[1]
    piece = pl.BlockSpec((TOK, TILE), lambda j, o: (0, j))
    block = WIDTH // YS
    return pl.pallas_call(
        functools.partial(weight_body, wide // TILE),
        grid_spec=pltpu.PrefetchScalarGridSpec(
            num_scalar_prefetch=1,
            grid=(wide // TILE,),
            in_specs=[pl.BlockSpec((WIDTH, SEQ), lambda j, o: (0, 0))] + [piece] * RANKS + hbm(len(after)),
            out_specs=[pl.BlockSpec((block, TILE), lambda j, o: (0, j))] * YS,
            scratch_shapes=[pltpu.VMEM((WIDTH, SEQ), F32), pltpu.VMEM((WIDTH, SEQ), F32)],
        ),
        out_shape=[jax.ShapeDtypeStruct((block, wide), BF16)] * YS,
        compiler_params=params(),
        cost_estimate=cost(2 * WIDTH * SEQ * wide, 2 * (WIDTH * SEQ + SEQ * wide + WIDTH * wide)),
        name="weight_grad",
    )(order, att, *pieces, *after)


def heads_body(count, carry, w_ref, *refs):
    acc_ref = refs[-1]
    out_ref = refs[-2]
    step = pl.program_id(0)

    @pl.when(step == 0)
    def _():
        acc_ref[...] = refs[RANKS][...] if carry else jnp.zeros_like(acc_ref)

    rows = jnp.concatenate([ref[...] for ref in refs[:RANKS]], axis=0)
    acc_ref[...] += dot(w_ref[...], rows, NT)

    @pl.when(step == count - 1)
    def _():
        out_ref[...] = acc_ref[...].astype(out_ref.dtype)


def heads_grad(weights, offset, pieces, carry, dtype, after=()):
    wide = pieces[0].shape[1]
    count = wide // TILE
    first = offset // TILE
    piece = pl.BlockSpec((TOK, TILE), lambda j: (0, j))
    whole = pl.BlockSpec((WIDTH, SEQ), lambda j: (0, 0))
    extra = [] if carry is None else [carry]
    return pl.pallas_call(
        functools.partial(heads_body, count, carry is not None),
        grid=(count,),
        in_specs=[pl.BlockSpec((WIDTH, TILE), lambda j: (0, j + first))]
        + [piece] * RANKS
        + [whole] * len(extra)
        + hbm(len(after)),
        out_specs=whole,
        out_shape=jax.ShapeDtypeStruct((WIDTH, SEQ), dtype),
        scratch_shapes=[pltpu.VMEM((WIDTH, SEQ), F32)],
        compiler_params=params(),
        cost_estimate=cost(2 * WIDTH * SEQ * wide, 2 * (WIDTH * SEQ + SEQ * wide + WIDTH * wide)),
        name="heads_grad",
    )(weights, *pieces, *extra, *after)


def rank(x, c):
    return (x % XS) * CS + c


ONWARD = [(rank(x, c), rank(x + 1 - 2 * c, c)) for x in range(XS) for c in range(CS)]
SIBLING = [(rank(x, c), rank(x, 1 - c)) for x in range(XS) for c in range(CS)]


def gather_rows(own):
    seq = ("x", "c")
    send = lambda value, perm: lax.ppermute(value, seq, perm)
    near = send(own, ONWARD)
    sib = send(own, SIBLING)
    near_sib = send(sib, ONWARD)
    far = send(near, ONWARD)
    back = send(near, SIBLING)
    back_sib = send(near_sib, SIBLING)
    far_sib = send(far, SIBLING)
    return [own, sib, near, near_sib, back, back_sib, far, far_sib]


def source(slot, x, c):
    step = 1 - 2 * c
    dx = (0, 0, -step, -step, step, step, 2, 2)[slot]
    other = (0, 1, 0, 1, 1, 0, 0, 1)[slot]
    return (x + dx + XS) % XS * CS + (c + other) % CS


def target(slot, x, c):
    return source({2: 5, 5: 2}.get(slot, slot), x, c)


PLACES = [(x, c) for x in range(XS) for c in range(CS)]
INWARD = [[(source(s, x, c), rank(x, c)) for x, c in PLACES] for s in range(RANKS)]
OUTWARD = [[(rank(x, c), source(s, x, c)) for x, c in PLACES] for s in range(RANKS)]


def targets_table():
    x, c = lax.axis_index("x"), lax.axis_index("c")
    return jnp.stack([target(s, x, c) for s in range(RANKS)]).astype(jnp.int32)


def clip_order():
    y, z = lax.axis_index("y"), lax.axis_index("z")
    return jnp.stack(
        [(y + i) % YS * ZS + (z + j) % ZS for i in range(YS) for j in range(ZS)]
    ).astype(jnp.int32)


def swap(pieces, perms):
    return [pieces[0]] + [lax.ppermute(p, ("x", "c"), q) for p, q in zip(pieces[1:], perms[1:])]


def around(parts, axis, size):
    return [parts[0]] + [
        lax.ppermute(parts[i], axis, [(a, (a + i) % size) for a in range(size)]) for i in range(1, size)
    ]


def total(parts):
    return functools.reduce(jnp.add, [p.astype(F32) for p in parts])


def scatter_sum(parts):
    row = WIDTH // (YS * ZS)
    part = total(around(parts, "y", YS)).astype(BF16)
    return total(around([part[i * row : (i + 1) * row] for i in range(ZS)], "z", ZS))


def local(queries, keys, values, cotangent, gate, w_out):
    targets = targets_table()
    order = clip_order()
    cot = cotangent[0, 0]
    mine = [cot[:, a : a + n] for a, n in zip(STARTS, CHUNKS)]
    other = [lax.ppermute(m, "b", [(0, 1)]) for m in mine]
    weights = lax.all_gather(w_out[0], ("y", "z"), axis=0, tiled=True)
    qkv = swap(pack(targets, queries[0, 0], keys[0, 0], values[0, 0]), INWARD)
    pieces = [gather_rows(gated(gate[0], cot, o, a)) for o, a in zip(other, STARTS)]
    prob, att = forward(qkv)
    terms = [weight_grad(order, att, pieces[0])]
    carry = heads_grad(weights, STARTS[0], pieces[0], None, F32, after=terms[-1][:1])
    for a, p in zip(STARTS[1:], pieces[1:]):
        terms.append(weight_grad(order, att, p, after=[carry]))
        last = a == STARTS[-1]
        carry = heads_grad(weights, a, p, carry, BF16 if last else F32, after=terms[-1][:1])
    grad_weight = [scatter_sum(t) for t in terms]
    groups, after = [], ()
    for first, count in GROUPS:
        home = backward(qkv, prob, carry, att, first, count, after)
        after = home[:1]
        groups.append(swap(home, OUTWARD))
    dq, dk, dv = unpack(targets, groups)
    return (
        dq[None, None],
        dk[None, None],
        dv[None, None],
        jnp.concatenate(grad_weight, axis=1)[None],
    )


def solution(mesh):
    fine = Mesh(mesh.devices.reshape(2, XS, CS, YS, ZS), ("b", "x", "c", "y", "z"))
    tokens = P("b", ("y", "z"), ("x", "c"), None)
    weight = P("b", ("x", "c", "y", "z"), None)
    return jax.shard_map(
        local,
        mesh=fine,
        in_specs=(tokens, tokens, tokens, tokens, P("b", ("y", "z"), None), weight),
        out_specs=(tokens, tokens, tokens, weight),
        check_vma=False,
    )
```

```python
import functools

import jax
import jax.numpy as jnp
from jax import lax
from jax.experimental import pallas as pl
from jax.experimental.pallas import tpu as pltpu
from jax.sharding import Mesh, PartitionSpec as P

HD = 128
XS, CS, YS, ZS = 4, 2, 4, 4
RANKS = XS * CS
TOK = 128
SEQ = RANKS * TOK
NH = 3
WIDTH = NH * HD
D = 5120
TILE = 1024
SCALE = HD**-0.5
LOG2E = 1.4426950408889634
F32 = jnp.float32
BF16 = jnp.bfloat16
NT = (((1,), (1,)), ((), ()))
NN = (((1,), (0,)), ((), ()))
CHUNKS = (3072, 2048)
STARTS = tuple(sum(CHUNKS[:i]) for i in range(len(CHUNKS)))
ROW = WIDTH // (YS * ZS)
VMEM_LIMIT = 56 * 1024 * 1024


def dot(a, b, dims=NN):
    return lax.dot_general(a, b, dims, preferred_element_type=F32)


def params(**more):
    return pltpu.CompilerParams(vmem_limit_bytes=VMEM_LIMIT, **more)


def cost(flops, nbytes, trans=0):
    return pl.CostEstimate(flops=flops, bytes_accessed=nbytes, transcendentals=trans)


def hbm(count):
    return [pl.BlockSpec(memory_space=pl.ANY)] * count


def pack_body(q_ref, k_ref, v_ref, out_ref):
    for r in range(RANKS):
        for i, ref in enumerate((q_ref, k_ref, v_ref)):
            out_ref[r, i] = ref[:, r * WIDTH : (r + 1) * WIDTH]


def pack(q, k, v):
    whole = pl.BlockSpec((TOK, RANKS * WIDTH), lambda j: (0, 0))
    return pl.pallas_call(
        pack_body,
        grid=(1,),
        in_specs=[whole] * 3,
        out_specs=pl.BlockSpec((RANKS, 3, TOK, WIDTH), lambda j: (0, 0, 0, 0)),
        out_shape=jax.ShapeDtypeStruct((RANKS, 3, TOK, WIDTH), BF16),
        compiler_params=params(),
        cost_estimate=cost(0, 2 * 3 * 2 * SEQ * WIDTH),
        name="pack",
    )(q, k, v)


def unpack_body(home_ref, *outs):
    for r in range(RANKS):
        for i, out in enumerate(outs):
            out[:, r * WIDTH : (r + 1) * WIDTH] = home_ref[r, i]


def unpack(home):
    whole = pl.BlockSpec((TOK, RANKS * WIDTH), lambda j: (0, 0))
    return pl.pallas_call(
        unpack_body,
        grid=(1,),
        in_specs=[pl.BlockSpec(home.shape, lambda j: (0, 0, 0, 0))],
        out_specs=[whole] * 3,
        out_shape=[jax.ShapeDtypeStruct((TOK, RANKS * WIDTH), BF16)] * 3,
        compiler_params=params(),
        cost_estimate=cost(0, 2 * 3 * 2 * SEQ * WIDTH),
        name="unpack",
    )(home)


def gate_body(gate_ref, mine_ref, other_ref, *refs):
    out_ref = refs[-1]
    total = mine_ref[...].astype(F32) + other_ref[...].astype(F32)
    out_ref[...] = (gate_ref[...] * total).astype(BF16)


def gated(gate, cot, other, start, after=()):
    wide = other.shape[1]
    at = start // TILE
    return pl.pallas_call(
        gate_body,
        grid=(wide // TILE,),
        in_specs=[
            pl.BlockSpec((1, TILE), lambda j: (0, j + at)),
            pl.BlockSpec((TOK, TILE), lambda j: (0, j + at)),
            pl.BlockSpec((TOK, TILE), lambda j: (0, j)),
        ]
        + hbm(len(after)),
        out_specs=pl.BlockSpec((TOK, TILE), lambda j: (0, j)),
        out_shape=jax.ShapeDtypeStruct((TOK, wide), BF16),
        compiler_params=params(),
        cost_estimate=cost(2 * TOK * wide, 6 * TOK * wide),
        name="gated",
    )(gate, cot, other, *after)


def forward_body(slot_ref, qkv_ref, *refs):
    prob_ref, att_ref, q_s, k_s, vt_s = refs[-5:]
    for s in range(RANKS):
        rows = pl.ds(s * TOK, TOK)
        piece = slot_ref[s]
        q_s[rows, :] = qkv_ref[piece, 0]
        k_s[rows, :] = qkv_ref[piece, 1]
        vt_s[:, rows] = qkv_ref[piece, 2].astype(F32).T.astype(BF16)
    scores = dot(k_s[...], q_s[...], NT)
    top = jnp.max(scores, axis=0, keepdims=True)
    e = jnp.exp2((scores - top) * (SCALE * LOG2E))
    norm = 1.0 / jnp.sum(e, axis=0, keepdims=True)
    prob = (e * norm).astype(BF16)
    prob_ref[0] = prob
    att_ref[...] = dot(vt_s[...], prob).astype(BF16)


def forward(slots, qkv, after=()):
    return pl.pallas_call(
        forward_body,
        grid_spec=pltpu.PrefetchScalarGridSpec(
            num_scalar_prefetch=1,
            grid=(NH,),
            in_specs=[pl.BlockSpec((RANKS, 3, TOK, HD), lambda h, s: (0, 0, 0, h))] + hbm(len(after)),
            out_specs=[
                pl.BlockSpec((1, SEQ, SEQ), lambda h, s: (h, 0, 0)),
                pl.BlockSpec((HD, SEQ), lambda h, s: (h, 0)),
            ],
            scratch_shapes=[
                pltpu.VMEM((SEQ, HD), BF16),
                pltpu.VMEM((SEQ, HD), BF16),
                pltpu.VMEM((HD, SEQ), BF16),
            ],
        ),
        out_shape=[
            jax.ShapeDtypeStruct((NH, SEQ, SEQ), BF16),
            jax.ShapeDtypeStruct((WIDTH, SEQ), BF16),
        ],
        compiler_params=params(),
        cost_estimate=cost(4 * NH * SEQ * SEQ * HD, 2 * NH * SEQ * SEQ + 8 * SEQ * WIDTH, NH * SEQ * SEQ),
        name="forward",
    )(slots, qkv, *after)


def backward_body(slot_ref, qkv_ref, prob_ref, gt_ref, att_ref, *refs):
    out_ref, q_s, v_s, kt_s = refs[-4:]
    for s in range(RANKS):
        rows = pl.ds(s * TOK, TOK)
        piece = slot_ref[s]
        q_s[rows, :] = qkv_ref[piece, 0]
        kt_s[:, rows] = qkv_ref[piece, 1].astype(F32).T.astype(BF16)
        v_s[rows, :] = qkv_ref[piece, 2]
    gt = gt_ref[...]
    prob = prob_ref[0]
    delta = jnp.sum(gt.astype(F32) * att_ref[...].astype(F32), axis=0, keepdims=True)
    dprob = dot(v_s[...], gt)
    dscore = (prob.astype(F32) * ((dprob - delta) * SCALE)).astype(BF16)
    grads = (
        dot(kt_s[...], dscore).T.astype(BF16),
        dot(dscore, q_s[...]).astype(BF16),
        dot(prob, gt, NT).astype(BF16),
    )
    for s in range(RANKS):
        for i, grad in enumerate(grads):
            out_ref[slot_ref[s], i] = grad[s * TOK : (s + 1) * TOK]


def backward(slots, qkv, prob, gt, att):
    return pl.pallas_call(
        backward_body,
        grid_spec=pltpu.PrefetchScalarGridSpec(
            num_scalar_prefetch=1,
            grid=(NH,),
            in_specs=[
                pl.BlockSpec((RANKS, 3, TOK, HD), lambda h, s: (0, 0, 0, h)),
                pl.BlockSpec((1, SEQ, SEQ), lambda h, s: (h, 0, 0)),
                pl.BlockSpec((HD, SEQ), lambda h, s: (h, 0)),
                pl.BlockSpec((HD, SEQ), lambda h, s: (h, 0)),
            ],
            out_specs=pl.BlockSpec((RANKS, 3, TOK, HD), lambda h, s: (0, 0, 0, h)),
            scratch_shapes=[
                pltpu.VMEM((SEQ, HD), BF16),
                pltpu.VMEM((SEQ, HD), BF16),
                pltpu.VMEM((HD, SEQ), BF16),
            ],
        ),
        out_shape=jax.ShapeDtypeStruct((RANKS, 3, TOK, WIDTH), BF16),
        compiler_params=params(),
        cost_estimate=cost(8 * NH * SEQ * SEQ * HD, 2 * NH * SEQ * (SEQ + 8 * HD)),
        name="backward",
    )(slots, qkv, prob, gt, att)


def row_specs(pieces, index):
    return [pl.BlockSpec((p.shape[0], TILE), index) for p in pieces]


def weight_body(parts, at_ref, att_ref, *refs):
    outs, wide_s, att_s = refs[-2 - YS : -2], refs[-2], refs[-1]
    block, row = WIDTH // YS, WIDTH // (YS * ZS)

    @pl.when(pl.program_id(0) == 0)
    def _():
        wide_s[...] = att_ref[...].astype(F32)
        for i in range(YS * ZS):
            start = pl.multiple_of(at_ref[i] * row, 8)
            att_s[pl.ds(i * row, row), :] = wide_s[pl.ds(start, row), :]

    rows = jnp.concatenate([ref[...] for ref in refs[:parts]], axis=0)
    term = dot(att_s[...].astype(BF16), rows).astype(BF16)
    for i, out in enumerate(outs):
        out[...] = term[i * block : (i + 1) * block]


def weight_grad(order, att, pieces, after=()):
    wide = pieces[0].shape[1]
    block = WIDTH // YS
    return pl.pallas_call(
        functools.partial(weight_body, len(pieces)),
        grid_spec=pltpu.PrefetchScalarGridSpec(
            num_scalar_prefetch=1,
            grid=(wide // TILE,),
            in_specs=[pl.BlockSpec((WIDTH, SEQ), lambda j, o: (0, 0))] + row_specs(pieces, lambda j, o: (0, j)) + hbm(len(after)),
            out_specs=[pl.BlockSpec((block, TILE), lambda j, o: (0, j))] * YS,
            scratch_shapes=[pltpu.VMEM((WIDTH, SEQ), F32), pltpu.VMEM((WIDTH, SEQ), F32)],
        ),
        out_shape=[jax.ShapeDtypeStruct((block, wide), BF16)] * YS,
        compiler_params=params(),
        cost_estimate=cost(2 * WIDTH * SEQ * wide, 2 * (WIDTH * SEQ + SEQ * wide + WIDTH * wide)),
        name="weight_grad",
    )(order, att, *pieces, *after)


def heads_body(count, parts, carry, from_ref, w_ref, *refs):
    acc_s, out_s = refs[-2:]
    out_ref = refs[-3]
    step = pl.program_id(0)

    @pl.when(step == 0)
    def _():
        acc_s[...] = refs[parts][...] if carry else jnp.zeros_like(acc_s)

    rows = jnp.concatenate([ref[...] for ref in refs[:parts]], axis=0)
    acc_s[...] += dot(w_ref[...], rows, NT)

    @pl.when(step == count - 1)
    def _():
        if carry:
            for i in range(YS * ZS):
                start = pl.multiple_of(from_ref[i] * ROW, 8)
                out_s[pl.ds(start, ROW), :] = acc_s[pl.ds(i * ROW, ROW), :]
            out_ref[...] = out_s[...].astype(BF16)
        else:
            out_ref[...] = acc_s[...]


def heads_grad(come, weights, offset, pieces, carry=None, after=()):
    wide = pieces[0].shape[1]
    count = wide // TILE
    first = offset // TILE
    whole = pl.BlockSpec((WIDTH, SEQ), lambda j, o: (0, 0))
    extra = [] if carry is None else [carry]
    return pl.pallas_call(
        functools.partial(heads_body, count, len(pieces), carry is not None),
        grid_spec=pltpu.PrefetchScalarGridSpec(
            num_scalar_prefetch=1,
            grid=(count,),
            in_specs=[pl.BlockSpec((WIDTH, TILE), lambda j, o: (0, j + first))]
            + row_specs(pieces, lambda j, o: (0, j))
            + [whole] * len(extra)
            + hbm(len(after)),
            out_specs=whole,
            scratch_shapes=[pltpu.VMEM((WIDTH, SEQ), F32), pltpu.VMEM((WIDTH, SEQ), F32)],
        ),
        out_shape=jax.ShapeDtypeStruct((WIDTH, SEQ), F32 if carry is None else BF16),
        compiler_params=params(),
        cost_estimate=cost(2 * WIDTH * SEQ * wide, 2 * (WIDTH * SEQ + SEQ * wide + WIDTH * wide)),
        name="heads_grad",
    )(come, weights, *pieces, *extra, *after)


def rank(x, c):
    return (x % XS) * CS + c


ONWARD = [(rank(x, c), rank(x + 1 - 2 * c, c)) for x in range(XS) for c in range(CS)]
SIBLING = [(rank(x, c), rank(x, 1 - c)) for x in range(XS) for c in range(CS)]


def send(value, perm):
    return lax.ppermute(value, ("x", "c"), perm)


def hold_body(*refs):
    pass


def hold(value, *after):
    return pl.pallas_call(
        hold_body,
        in_specs=hbm(1 + len(after)),
        out_specs=hbm(1)[0],
        out_shape=jax.ShapeDtypeStruct(value.shape, value.dtype),
        input_output_aliases={0: 0},
        compiler_params=params(),
        cost_estimate=cost(0, 0),
        name="hold",
    )(value, *after)


def slot_table():
    x, c = lax.axis_index("x"), lax.axis_index("c")
    step = 1 - 2 * c
    at = lambda xx, cc: lax.rem(xx + 2 * XS, XS) * CS + cc
    return jnp.stack(
        [
            at(x, c),
            at(x, 1 - c),
            at(x - step, c),
            at(x - step, 1 - c),
            at(x + step, 1 - c),
            at(x + step, c),
            at(x + 2, c),
            at(x + 2, 1 - c),
        ]
    ).astype(jnp.int32)


def exchange(value, axis):
    return lax.all_to_all(value, axis, split_axis=0, concat_axis=0, tiled=True)


def clip_order():
    y, z = lax.axis_index("y"), lax.axis_index("z")
    return jnp.stack([(y + i) % YS * ZS + (z + j) % ZS for i in range(YS) for j in range(ZS)]).astype(jnp.int32)


def come_order():
    z = lax.axis_index("z")
    return jnp.stack([i * ZS + (z - j + ZS) % ZS for i in range(YS) for j in range(ZS)]).astype(jnp.int32)


def around(parts, axis, size):
    return [parts[0]] + [
        lax.ppermute(parts[i], axis, [(a, (a + i) % size) for a in range(size)]) for i in range(1, size)
    ]


def total(parts):
    return functools.reduce(jnp.add, [p.astype(F32) for p in parts])


def scatter_sum(parts, *after):
    got = around(parts, "y", YS)
    if after:
        got[1] = hold(got[1], *after)
    part = total(got).astype(BF16)
    return total(around([part[i * ROW : (i + 1) * ROW] for i in range(ZS)], "z", ZS))


def local(queries, keys, values, cotangent, gate, w_out):
    slots = slot_table()
    order, come = clip_order(), come_order()
    cot = cotangent[0, 0]
    to_context = lambda value: lax.ppermute(value, "b", [(0, 1)])

    other0 = to_context(cot[:, : CHUNKS[0]])
    packed = pack(queries[0, 0], keys[0, 0], values[0, 0])
    qkv = exchange(packed, ("x", "c"))
    along_z = around([w_out[0]] * ZS, "z", ZS)
    along_z[1] = hold(along_z[1], other0, qkv)
    along_z = jnp.concatenate(along_z, axis=0)
    weights = lax.all_gather(along_z, "y", axis=0, tiled=True)
    own0 = gated(gate[0], cot, other0, STARTS[0], after=[along_z])
    near0 = send(own0, ONWARD)
    sib0 = send(own0, SIBLING)
    near_sib0 = send(sib0, ONWARD)
    other1 = to_context(hold(cot[:, STARTS[1] :], other0))
    prob, att = forward(slots, qkv, after=[sib0])
    own1 = gated(gate[0], cot, other1, STARTS[1], after=[att])
    near1 = send(own1, ONWARD)
    sib1 = send(own1, SIBLING)
    near_sib1 = send(sib1, ONWARD)
    near0 = hold(near0, sib1)
    far0 = hold(send(near0, ONWARD), near1)
    pieces0 = [own0, sib0, near0, near_sib0, send(near0, SIBLING), send(near_sib0, SIBLING), far0, send(far0, SIBLING)]
    far1 = send(near1, ONWARD)
    first_term = weight_grad(order, att, pieces0)
    acc = heads_grad(come, weights, 0, pieces0, after=[first_term[0]])
    far1 = hold(far1, acc)
    pieces1 = [own1, sib1, near1, near_sib1, send(near1, SIBLING), send(near_sib1, SIBLING), far1, send(far1, SIBLING)]
    gt = heads_grad(come, weights, STARTS[1], pieces1, acc)
    home = backward(slots, qkv, prob, gt, att)
    last_term = weight_grad(order, att, pieces1, after=[home])
    first_sum = scatter_sum(first_term, last_term[0])
    last_sum = scatter_sum(last_term)
    dq, dk, dv = unpack(exchange(home, ("x", "c")))
    return (
        dq[None, None],
        dk[None, None],
        dv[None, None],
        jnp.concatenate([first_sum, last_sum], axis=1)[None],
    )


def solution(mesh):
    fine = Mesh(mesh.devices.reshape(2, XS, CS, YS, ZS), ("b", "x", "c", "y", "z"))
    tokens = P("b", ("y", "z"), ("x", "c"), None)
    weight = P("b", ("x", "c", "y", "z"), None)
    return jax.shard_map(
        local,
        mesh=fine,
        in_specs=(tokens, tokens, tokens, tokens, P("b", ("y", "z"), None), weight),
        out_specs=(tokens, tokens, tokens, weight),
        check_vma=False,
    )
```

```python
import functools

import jax
import jax.numpy as jnp
from jax import lax
from jax.experimental import pallas as pl
from jax.experimental.pallas import tpu as pltpu
from jax.sharding import Mesh, PartitionSpec as P

HD = 128
XS, CS, YS, ZS = 4, 2, 4, 4
RANKS = XS * CS
TOK = 128
SEQ = RANKS * TOK
NH = 3
WIDTH = NH * HD
D = 5120
TILE = 1024
GATE_TILE = 2560
SCALE = HD**-0.5
LOG2E = 1.4426950408889634
F32 = jnp.float32
BF16 = jnp.bfloat16
NT = (((1,), (1,)), ((), ()))
NN = (((1,), (0,)), ((), ()))
CHUNKS = (3072, 2048)
STARTS = tuple(sum(CHUNKS[:i]) for i in range(len(CHUNKS)))
ROW = WIDTH // (YS * ZS)
BLOCK = WIDTH // YS
VMEM_LIMIT = 56 * 1024 * 1024


def dot(a, b, dims=NN):
    return lax.dot_general(a, b, dims, preferred_element_type=F32)


def params(**more):
    return pltpu.CompilerParams(vmem_limit_bytes=VMEM_LIMIT, **more)


def cost(flops, nbytes, trans=0):
    return pl.CostEstimate(flops=flops, bytes_accessed=nbytes, transcendentals=trans)


def hbm(count):
    return [pl.BlockSpec(memory_space=pl.ANY)] * count


def pack_body(q_ref, k_ref, v_ref, out_ref):
    for r in range(RANKS):
        for i, ref in enumerate((q_ref, k_ref, v_ref)):
            out_ref[r, i] = ref[:, r * WIDTH : (r + 1) * WIDTH]


def pack(q, k, v):
    whole = pl.BlockSpec((TOK, RANKS * WIDTH), lambda j: (0, 0))
    return pl.pallas_call(
        pack_body,
        grid=(1,),
        in_specs=[whole] * 3,
        out_specs=pl.BlockSpec((RANKS, 3, TOK, WIDTH), lambda j: (0, 0, 0, 0)),
        out_shape=jax.ShapeDtypeStruct((RANKS, 3, TOK, WIDTH), BF16),
        compiler_params=params(),
        cost_estimate=cost(0, 2 * 3 * 2 * SEQ * WIDTH),
        name="pack",
    )(q, k, v)


def unpack_body(home_ref, *outs):
    for r in range(RANKS):
        for i, out in enumerate(outs):
            out[:, r * WIDTH : (r + 1) * WIDTH] = home_ref[r, i]


def unpack(home):
    whole = pl.BlockSpec((TOK, RANKS * WIDTH), lambda j: (0, 0))
    return pl.pallas_call(
        unpack_body,
        grid=(1,),
        in_specs=[pl.BlockSpec(home.shape, lambda j: (0, 0, 0, 0))],
        out_specs=[whole] * 3,
        out_shape=[jax.ShapeDtypeStruct((TOK, RANKS * WIDTH), BF16)] * 3,
        compiler_params=params(),
        cost_estimate=cost(0, 2 * 3 * 2 * SEQ * WIDTH),
        name="unpack",
    )(home)


def gate_body(gate_ref, mine_ref, other_ref, *refs):
    out_ref = refs[-1]
    total = mine_ref[...].astype(F32) + other_ref[...].astype(F32)
    out_ref[...] = (gate_ref[...] * total).astype(BF16)


def gated(gate, cot, other, start, wide, after=()):
    at = start // GATE_TILE
    return pl.pallas_call(
        gate_body,
        grid=(wide // GATE_TILE,),
        in_specs=[
            pl.BlockSpec((1, GATE_TILE), lambda j: (0, j + at)),
            pl.BlockSpec((TOK, GATE_TILE), lambda j: (0, j + at)),
            pl.BlockSpec((TOK, GATE_TILE), lambda j: (0, j + at)),
        ]
        + hbm(len(after)),
        out_specs=pl.BlockSpec((TOK, GATE_TILE), lambda j: (0, j)),
        out_shape=jax.ShapeDtypeStruct((TOK, wide), BF16),
        compiler_params=params(),
        cost_estimate=cost(2 * TOK * wide, 6 * TOK * wide),
        name="gated",
    )(gate, cot, other, *after)


def forward_body(slot_ref, qkv_ref, *refs):
    prob_ref, att_ref, q_s, k_s, vt_s = refs[-5:]
    for s in range(RANKS):
        rows = pl.ds(s * TOK, TOK)
        piece = slot_ref[s]
        q_s[rows, :] = qkv_ref[piece, 0]
        k_s[rows, :] = qkv_ref[piece, 1]
        vt_s[:, rows] = qkv_ref[piece, 2].astype(F32).T.astype(BF16)
    scores = dot(k_s[...], q_s[...], NT)
    top = jnp.max(scores, axis=0, keepdims=True)
    e = jnp.exp2((scores - top) * (SCALE * LOG2E))
    norm = 1.0 / jnp.sum(e, axis=0, keepdims=True)
    prob = (e * norm).astype(BF16)
    prob_ref[0] = prob
    att_ref[...] = dot(vt_s[...], prob).astype(BF16)


def forward(slots, qkv, after=()):
    return pl.pallas_call(
        forward_body,
        grid_spec=pltpu.PrefetchScalarGridSpec(
            num_scalar_prefetch=1,
            grid=(NH,),
            in_specs=[pl.BlockSpec((RANKS, 3, TOK, HD), lambda h, s: (0, 0, 0, h))] + hbm(len(after)),
            out_specs=[
                pl.BlockSpec((1, SEQ, SEQ), lambda h, s: (h, 0, 0)),
                pl.BlockSpec((HD, SEQ), lambda h, s: (h, 0)),
            ],
            scratch_shapes=[
                pltpu.VMEM((SEQ, HD), BF16),
                pltpu.VMEM((SEQ, HD), BF16),
                pltpu.VMEM((HD, SEQ), BF16),
            ],
        ),
        out_shape=[
            jax.ShapeDtypeStruct((NH, SEQ, SEQ), BF16),
            jax.ShapeDtypeStruct((WIDTH, SEQ), BF16),
        ],
        compiler_params=params(),
        cost_estimate=cost(4 * NH * SEQ * SEQ * HD, 2 * NH * SEQ * SEQ + 8 * SEQ * WIDTH, NH * SEQ * SEQ),
        name="forward",
    )(slots, qkv, *after)


def backward_body(slot_ref, qkv_ref, prob_ref, gt_ref, att_ref, *refs):
    out_ref, q_s, v_s, kt_s = refs[-4:]
    for s in range(RANKS):
        rows = pl.ds(s * TOK, TOK)
        piece = slot_ref[s]
        q_s[rows, :] = qkv_ref[piece, 0]
        kt_s[:, rows] = qkv_ref[piece, 1].astype(F32).T.astype(BF16)
        v_s[rows, :] = qkv_ref[piece, 2]
    gt = gt_ref[...]
    prob = prob_ref[0]
    delta = jnp.sum(gt.astype(F32) * att_ref[...].astype(F32), axis=0, keepdims=True)
    dprob = dot(v_s[...], gt)
    dscore = (prob.astype(F32) * ((dprob - delta) * SCALE)).astype(BF16)
    grads = (
        dot(kt_s[...], dscore).T.astype(BF16),
        dot(dscore, q_s[...]).astype(BF16),
        dot(prob, gt, NT).astype(BF16),
    )
    for s in range(RANKS):
        for i, grad in enumerate(grads):
            out_ref[slot_ref[s], i] = grad[s * TOK : (s + 1) * TOK]


def backward(slots, qkv, prob, gt, att):
    return pl.pallas_call(
        backward_body,
        grid_spec=pltpu.PrefetchScalarGridSpec(
            num_scalar_prefetch=1,
            grid=(NH,),
            in_specs=[
                pl.BlockSpec((RANKS, 3, TOK, HD), lambda h, s: (0, 0, 0, h)),
                pl.BlockSpec((1, SEQ, SEQ), lambda h, s: (h, 0, 0)),
                pl.BlockSpec((HD, SEQ), lambda h, s: (h, 0)),
                pl.BlockSpec((HD, SEQ), lambda h, s: (h, 0)),
            ],
            out_specs=pl.BlockSpec((RANKS, 3, TOK, HD), lambda h, s: (0, 0, 0, h)),
            scratch_shapes=[
                pltpu.VMEM((SEQ, HD), BF16),
                pltpu.VMEM((SEQ, HD), BF16),
                pltpu.VMEM((HD, SEQ), BF16),
            ],
        ),
        out_shape=jax.ShapeDtypeStruct((RANKS, 3, TOK, WIDTH), BF16),
        compiler_params=params(),
        cost_estimate=cost(8 * NH * SEQ * SEQ * HD, 2 * NH * SEQ * (SEQ + 8 * HD)),
        name="backward",
    )(slots, qkv, prob, gt, att)


def row_specs(pieces, index):
    return [pl.BlockSpec((p.shape[0], TILE), index) for p in pieces]


def weight_body(parts, at_ref, att_ref, *refs):
    out_ref, wide_s, att_s = refs[-3:]
    row = ROW

    @pl.when(pl.program_id(0) == 0)
    def _():
        wide_s[...] = att_ref[...].astype(F32)
        for i in range(YS * ZS):
            start = pl.multiple_of(at_ref[i] * row, 8)
            att_s[pl.ds(i * row, row), :] = wide_s[pl.ds(start, row), :]

    rows = jnp.concatenate([ref[...] for ref in refs[:parts]], axis=0)
    term = dot(att_s[...].astype(BF16), rows).astype(BF16)
    for i in range(YS):
        out_ref[i] = term[i * BLOCK : (i + 1) * BLOCK]


def weight_grad(order, att, pieces, after=()):
    wide = pieces[0].shape[1]
    return pl.pallas_call(
        functools.partial(weight_body, len(pieces)),
        grid_spec=pltpu.PrefetchScalarGridSpec(
            num_scalar_prefetch=1,
            grid=(wide // TILE,),
            in_specs=[pl.BlockSpec((WIDTH, SEQ), lambda j, o: (0, 0))] + row_specs(pieces, lambda j, o: (0, j)) + hbm(len(after)),
            out_specs=pl.BlockSpec((YS, BLOCK, TILE), lambda j, o: (0, 0, j)),
            scratch_shapes=[pltpu.VMEM((WIDTH, SEQ), F32), pltpu.VMEM((WIDTH, SEQ), F32)],
        ),
        out_shape=jax.ShapeDtypeStruct((YS, BLOCK, wide), BF16),
        compiler_params=params(),
        cost_estimate=cost(2 * WIDTH * SEQ * wide, 2 * (WIDTH * SEQ + SEQ * wide + WIDTH * wide)),
        name="weight_grad",
    )(order, att, *pieces, *after)


def heads_body(counts, parts, w_ref, *refs):
    out_ref, acc_s = refs[-2:]
    step = pl.program_id(0)

    @pl.when(step == 0)
    def _():
        acc_s[...] = jnp.zeros_like(acc_s)

    begin = 0
    for i, count in enumerate(counts):
        pieces = refs[i * parts : (i + 1) * parts]

        @pl.when((step >= begin) & (step < begin + count))
        def _():
            rows = jnp.concatenate([ref[...] for ref in pieces], axis=0)
            acc_s[...] += dot(w_ref[...], rows, NT)

        begin += count

    @pl.when(step == begin - 1)
    def _():
        out_ref[...] = acc_s[...].astype(BF16)


def heads_grad(weights, groups, after=()):
    counts = [g[0].shape[1] // TILE for g in groups]
    first, last = counts
    near = lambda j: (0, jnp.minimum(j, first - 1))
    far = lambda j: (0, jnp.maximum(j - first, 0))
    return pl.pallas_call(
        functools.partial(heads_body, counts, len(groups[0])),
        grid=(first + last,),
        in_specs=[pl.BlockSpec((WIDTH, TILE), lambda j: (0, j))]
        + row_specs(groups[0], near)
        + row_specs(groups[1], far)
        + hbm(len(after)),
        out_specs=pl.BlockSpec((WIDTH, SEQ), lambda j: (0, 0)),
        scratch_shapes=[pltpu.VMEM((WIDTH, SEQ), F32)],
        out_shape=jax.ShapeDtypeStruct((WIDTH, SEQ), BF16),
        compiler_params=params(),
        cost_estimate=cost(2 * WIDTH * SEQ * D, 2 * (WIDTH * SEQ + SEQ * D + WIDTH * D)),
        name="heads_grad",
    )(weights, *groups[0], *groups[1], *after)


def rank(x, c):
    return (x % XS) * CS + c


ONWARD = [(rank(x, c), rank(x + 1 - 2 * c, c)) for x in range(XS) for c in range(CS)]
SIBLING = [(rank(x, c), rank(x, 1 - c)) for x in range(XS) for c in range(CS)]


def send(value, perm):
    return lax.ppermute(value, ("x", "c"), perm)


def hold_body(*refs):
    pass


def hold(value, *after):
    return pl.pallas_call(
        hold_body,
        in_specs=hbm(1 + len(after)),
        out_specs=hbm(1)[0],
        out_shape=jax.ShapeDtypeStruct(value.shape, value.dtype),
        input_output_aliases={0: 0},
        compiler_params=params(),
        cost_estimate=cost(0, 0),
        name="hold",
    )(value, *after)


def pair_body(own_ref, sib_ref, *refs):
    out_ref = refs[-1]
    out_ref[:TOK] = own_ref[...]
    out_ref[TOK:] = sib_ref[...]


def pair_up(own, sib, start, wide, after):
    at = start // TILE
    spec = pl.BlockSpec((TOK, TILE), lambda j: (0, j + at))
    return pl.pallas_call(
        pair_body,
        grid=(wide // TILE,),
        in_specs=[spec] * 2 + hbm(len(after)),
        out_specs=pl.BlockSpec((2 * TOK, TILE), lambda j: (0, j)),
        out_shape=jax.ShapeDtypeStruct((2 * TOK, wide), BF16),
        compiler_params=params(),
        cost_estimate=cost(0, 8 * TOK * wide),
        name="pair_up",
    )(own, sib, *after)


def slot_table():
    x, c = lax.axis_index("x"), lax.axis_index("c")
    step = 1 - 2 * c
    at = lambda xx, cc: lax.rem(xx + 2 * XS, XS) * CS + cc
    return jnp.stack(
        [
            at(x, c),
            at(x, 1 - c),
            at(x - step, c),
            at(x - step, 1 - c),
            at(x + step, 1 - c),
            at(x + step, c),
            at(x + 2, c),
            at(x + 2, 1 - c),
        ]
    ).astype(jnp.int32)


def exchange(value, axis):
    return lax.all_to_all(value, axis, split_axis=0, concat_axis=0, tiled=True)


def clip_order(seen):
    y, z = seen * lax.axis_index("y"), lax.axis_index("z")
    return jnp.stack([(y + i) % YS * ZS + (z + j) % ZS for i in range(YS) for j in range(ZS)]).astype(jnp.int32)


def around(parts, axis, size):
    return [parts[0]] + [
        lax.ppermute(parts[i], axis, [(a, (a + i) % size) for a in range(size)]) for i in range(1, size)
    ]


def total(parts):
    return functools.reduce(jnp.add, [p.astype(F32) for p in parts])


def scatter_sum(part):
    part = part.astype(BF16)
    return total(around([part[i * ROW : (i + 1) * ROW] for i in range(ZS)], "z", ZS))


def local(queries, keys, values, cotangent, gate, w_out):
    slots = slot_table()
    cot = cotangent[0, 0]
    to_context = lambda value: lax.ppermute(value, "b", [(0, 1)])

    other = to_context(cot)
    packed = pack(queries[0, 0], keys[0, 0], values[0, 0])
    qkv = exchange(packed, ("x", "c"))
    own = gated(gate[0], cot, other, 0, D, after=[packed])
    sib = send(own, SIBLING)
    weights = lax.all_gather(hold(w_out[0], sib, qkv), ("y", "z"), axis=0, tiled=True)
    pair0 = pair_up(own, sib, STARTS[0], CHUNKS[0], [])
    near0 = send(pair0, ONWARD)
    prob, att = forward(slots, qkv, after=[pair0])
    pair1 = pair_up(own, sib, STARTS[1], CHUNKS[1], [att])
    near1 = send(pair1, ONWARD)
    near0 = hold(near0, pair1)
    far0 = hold(send(near0[:TOK], ONWARD), near1)
    pieces0 = [pair0, near0, send(near0, SIBLING), far0, send(far0, SIBLING)]
    first_term = weight_grad(clip_order(0), att, pieces0)
    far1 = send(near1[:TOK], ONWARD)
    far1 = hold(far1, first_term)
    pieces1 = [pair1, near1, send(near1, SIBLING), far1, send(far1, SIBLING)]
    last_term = weight_grad(clip_order(1), att, pieces1)
    gt = heads_grad(weights, (pieces0, pieces1), after=[last_term])
    home = backward(slots, qkv, prob, gt, att)
    got = hold(exchange(first_term, "y"), home)
    last = around([last_term[i] for i in range(YS)], "y", YS)
    last[0] = hold(last[0], got)
    first_sum = scatter_sum(jnp.sum(got.astype(F32), axis=0))
    last_sum = scatter_sum(total(last))
    dq, dk, dv = unpack(exchange(home, ("x", "c")))
    return (
        dq[None, None],
        dk[None, None],
        dv[None, None],
        jnp.concatenate([first_sum, last_sum], axis=1)[None],
    )


def solution(mesh):
    fine = Mesh(mesh.devices.reshape(2, XS, CS, YS, ZS), ("b", "x", "c", "y", "z"))
    tokens = P("b", ("y", "z"), ("x", "c"), None)
    weight = P("b", ("x", "c", "y", "z"), None)
    return jax.shard_map(
        local,
        mesh=fine,
        in_specs=(tokens, tokens, tokens, tokens, P("b", ("y", "z"), None), weight),
        out_specs=(tokens, tokens, tokens, weight),
        check_vma=False,
    )
```

```python
import functools

import jax
import jax.numpy as jnp
from jax import lax
from jax.experimental import pallas as pl
from jax.experimental.pallas import tpu as pltpu
from jax.sharding import Mesh, PartitionSpec as P

HD = 128
XS, CS, YS, ZS = 4, 2, 4, 4
RANKS = XS * CS
TOK = 128
SEQ = RANKS * TOK
NH = 3
WIDTH = NH * HD
D = 5120
TILE = 1024
GATE_TILE = 2560
SCALE = HD**-0.5
LOG2E = 1.4426950408889634
F32 = jnp.float32
BF16 = jnp.bfloat16
NT = (((1,), (1,)), ((), ()))
NN = (((1,), (0,)), ((), ()))
CHUNKS = (2048, 3072)
STARTS = tuple(sum(CHUNKS[:i]) for i in range(len(CHUNKS)))
ROW = WIDTH // (YS * ZS)
BLOCK = WIDTH // YS
VMEM_LIMIT = 56 * 1024 * 1024


def dot(a, b, dims=NN):
    return lax.dot_general(a, b, dims, preferred_element_type=F32)


def params(**more):
    return pltpu.CompilerParams(vmem_limit_bytes=VMEM_LIMIT, **more)


def cost(flops, nbytes, trans=0):
    return pl.CostEstimate(flops=flops, bytes_accessed=nbytes, transcendentals=trans)


def hbm(count):
    return [pl.BlockSpec(memory_space=pl.ANY)] * count


def pack_body(q_ref, k_ref, v_ref, out_ref):
    for r in range(RANKS):
        for i, ref in enumerate((q_ref, k_ref, v_ref)):
            out_ref[r, i] = ref[:, r * WIDTH : (r + 1) * WIDTH]


def pack(q, k, v):
    whole = pl.BlockSpec((TOK, RANKS * WIDTH), lambda j: (0, 0))
    return pl.pallas_call(
        pack_body,
        grid=(1,),
        in_specs=[whole] * 3,
        out_specs=pl.BlockSpec((RANKS, 3, TOK, WIDTH), lambda j: (0, 0, 0, 0)),
        out_shape=jax.ShapeDtypeStruct((RANKS, 3, TOK, WIDTH), BF16),
        compiler_params=params(),
        cost_estimate=cost(0, 2 * 3 * 2 * SEQ * WIDTH),
        name="pack",
    )(q, k, v)


def unpack_body(home_ref, *outs):
    for r in range(RANKS):
        for i, out in enumerate(outs):
            out[:, r * WIDTH : (r + 1) * WIDTH] = home_ref[r, i]


def unpack(home):
    whole = pl.BlockSpec((TOK, RANKS * WIDTH), lambda j: (0, 0))
    return pl.pallas_call(
        unpack_body,
        grid=(1,),
        in_specs=[pl.BlockSpec(home.shape, lambda j: (0, 0, 0, 0))],
        out_specs=[whole] * 3,
        out_shape=[jax.ShapeDtypeStruct((TOK, RANKS * WIDTH), BF16)] * 3,
        compiler_params=params(),
        cost_estimate=cost(0, 2 * 3 * 2 * SEQ * WIDTH),
        name="unpack",
    )(home)


def gate_body(gate_ref, mine_ref, other_ref, *refs):
    out_ref = refs[-1]
    total = mine_ref[...].astype(F32) + other_ref[...].astype(F32)
    out_ref[...] = (gate_ref[...] * total).astype(BF16)


def gated(gate, cot, other, start, wide, after=()):
    at = start // GATE_TILE
    return pl.pallas_call(
        gate_body,
        grid=(wide // GATE_TILE,),
        in_specs=[
            pl.BlockSpec((1, GATE_TILE), lambda j: (0, j + at)),
            pl.BlockSpec((TOK, GATE_TILE), lambda j: (0, j + at)),
            pl.BlockSpec((TOK, GATE_TILE), lambda j: (0, j + at)),
        ]
        + hbm(len(after)),
        out_specs=pl.BlockSpec((TOK, GATE_TILE), lambda j: (0, j)),
        out_shape=jax.ShapeDtypeStruct((TOK, wide), BF16),
        compiler_params=params(),
        cost_estimate=cost(2 * TOK * wide, 6 * TOK * wide),
        name="gated",
    )(gate, cot, other, *after)


def forward_body(slot_ref, qkv_ref, *refs):
    prob_ref, att_ref, q_s, k_s, vt_s = refs[-5:]
    for s in range(RANKS):
        rows = pl.ds(s * TOK, TOK)
        piece = slot_ref[s]
        q_s[rows, :] = qkv_ref[piece, 0]
        k_s[rows, :] = qkv_ref[piece, 1]
        vt_s[:, rows] = qkv_ref[piece, 2].astype(F32).T.astype(BF16)
    scores = dot(k_s[...], q_s[...], NT)
    top = jnp.max(scores, axis=0, keepdims=True)
    e = jnp.exp2((scores - top) * (SCALE * LOG2E))
    norm = 1.0 / jnp.sum(e, axis=0, keepdims=True)
    prob = (e * norm).astype(BF16)
    prob_ref[0] = prob
    att_ref[...] = dot(vt_s[...], prob).astype(BF16)


def forward(slots, qkv, after=()):
    return pl.pallas_call(
        forward_body,
        grid_spec=pltpu.PrefetchScalarGridSpec(
            num_scalar_prefetch=1,
            grid=(NH,),
            in_specs=[pl.BlockSpec((RANKS, 3, TOK, HD), lambda h, s: (0, 0, 0, h))] + hbm(len(after)),
            out_specs=[
                pl.BlockSpec((1, SEQ, SEQ), lambda h, s: (h, 0, 0)),
                pl.BlockSpec((HD, SEQ), lambda h, s: (h, 0)),
            ],
            scratch_shapes=[
                pltpu.VMEM((SEQ, HD), BF16),
                pltpu.VMEM((SEQ, HD), BF16),
                pltpu.VMEM((HD, SEQ), BF16),
            ],
        ),
        out_shape=[
            jax.ShapeDtypeStruct((NH, SEQ, SEQ), BF16),
            jax.ShapeDtypeStruct((WIDTH, SEQ), BF16),
        ],
        compiler_params=params(),
        cost_estimate=cost(4 * NH * SEQ * SEQ * HD, 2 * NH * SEQ * SEQ + 8 * SEQ * WIDTH, NH * SEQ * SEQ),
        name="forward",
    )(slots, qkv, *after)


def backward_body(slot_ref, qkv_ref, prob_ref, gt_ref, att_ref, *refs):
    out_ref, q_s, v_s, kt_s = refs[-4:]
    for s in range(RANKS):
        rows = pl.ds(s * TOK, TOK)
        piece = slot_ref[s]
        q_s[rows, :] = qkv_ref[piece, 0]
        kt_s[:, rows] = qkv_ref[piece, 1].astype(F32).T.astype(BF16)
        v_s[rows, :] = qkv_ref[piece, 2]
    gt = gt_ref[...]
    prob = prob_ref[0]
    delta = jnp.sum(gt.astype(F32) * att_ref[...].astype(F32), axis=0, keepdims=True)
    dprob = dot(v_s[...], gt)
    dscore = (prob.astype(F32) * (dprob - delta)).astype(BF16)
    grads = (
        (dot(kt_s[...], dscore) * SCALE).T.astype(BF16),
        (dot(dscore, q_s[...]) * SCALE).astype(BF16),
        dot(prob, gt, NT).astype(BF16),
    )
    for s in range(RANKS):
        for i, grad in enumerate(grads):
            out_ref[slot_ref[s], i] = grad[s * TOK : (s + 1) * TOK]


def backward(slots, qkv, prob, gt, att):
    return pl.pallas_call(
        backward_body,
        grid_spec=pltpu.PrefetchScalarGridSpec(
            num_scalar_prefetch=1,
            grid=(NH,),
            in_specs=[
                pl.BlockSpec((RANKS, 3, TOK, HD), lambda h, s: (0, 0, 0, h)),
                pl.BlockSpec((1, SEQ, SEQ), lambda h, s: (h, 0, 0)),
                pl.BlockSpec((HD, SEQ), lambda h, s: (h, 0)),
                pl.BlockSpec((HD, SEQ), lambda h, s: (h, 0)),
            ],
            out_specs=pl.BlockSpec((RANKS, 3, TOK, HD), lambda h, s: (0, 0, 0, h)),
            scratch_shapes=[
                pltpu.VMEM((SEQ, HD), BF16),
                pltpu.VMEM((SEQ, HD), BF16),
                pltpu.VMEM((HD, SEQ), BF16),
            ],
        ),
        out_shape=jax.ShapeDtypeStruct((RANKS, 3, TOK, WIDTH), BF16),
        compiler_params=params(),
        cost_estimate=cost(8 * NH * SEQ * SEQ * HD, 2 * NH * SEQ * (SEQ + 8 * HD)),
        name="backward",
    )(slots, qkv, prob, gt, att)


def row_specs(pieces, index):
    return [pl.BlockSpec((p.shape[0], TILE), index) for p in pieces]


def weight_body(parts, count, at_ref, att_ref, *refs):
    outs, wide_s, att_s = refs[parts + count : -2], refs[-2], refs[-1]
    row = ROW

    @pl.when(pl.program_id(0) == 0)
    def _():
        wide_s[...] = att_ref[...].astype(F32)
        for i in range(YS * ZS):
            start = pl.multiple_of(at_ref[i] * row, 8)
            att_s[pl.ds(i * row, row), :] = wide_s[pl.ds(start, row), :]

    rows = jnp.concatenate([ref[...] for ref in refs[:parts]], axis=0)
    term = dot(att_s[...].astype(BF16), rows).astype(BF16)
    for i in range(YS):
        block = term[i * BLOCK : (i + 1) * BLOCK]
        if len(outs) == 1:
            outs[0][i] = block
        else:
            outs[i][...] = block


def weight_grad(order, att, pieces, split, after=()):
    wide = pieces[0].shape[1]
    return pl.pallas_call(
        functools.partial(weight_body, len(pieces), len(after)),
        grid_spec=pltpu.PrefetchScalarGridSpec(
            num_scalar_prefetch=1,
            grid=(wide // TILE,),
            in_specs=[pl.BlockSpec((WIDTH, SEQ), lambda j, o: (0, 0))] + row_specs(pieces, lambda j, o: (0, j)) + hbm(len(after)),
            out_specs=[pl.BlockSpec((BLOCK, TILE), lambda j, o: (0, j))] * YS
            if split
            else [pl.BlockSpec((YS, BLOCK, TILE), lambda j, o: (0, 0, j))],
            scratch_shapes=[pltpu.VMEM((WIDTH, SEQ), F32), pltpu.VMEM((WIDTH, SEQ), F32)],
        ),
        out_shape=[jax.ShapeDtypeStruct((BLOCK, wide), BF16)] * YS
        if split
        else [jax.ShapeDtypeStruct((YS, BLOCK, wide), BF16)],
        compiler_params=params(),
        cost_estimate=cost(2 * WIDTH * SEQ * wide, 2 * (WIDTH * SEQ + SEQ * wide + WIDTH * wide)),
        name="weight_grad",
    )(order, att, *pieces, *after)


def heads_body(counts, parts, w_ref, *refs):
    out_ref, acc_s = refs[-2:]
    step = pl.program_id(0)

    @pl.when(step == 0)
    def _():
        acc_s[...] = jnp.zeros_like(acc_s)

    begin = 0
    for i, count in enumerate(counts):
        pieces = refs[i * parts : (i + 1) * parts]

        @pl.when((step >= begin) & (step < begin + count))
        def _():
            rows = jnp.concatenate([ref[...] for ref in pieces], axis=0)
            acc_s[...] += dot(w_ref[...], rows, NT)

        begin += count

    @pl.when(step == begin - 1)
    def _():
        out_ref[...] = acc_s[...].astype(BF16)


def heads_grad(weights, groups, after=()):
    counts = [g[0].shape[1] // TILE for g in groups]
    first, last = counts
    near = lambda j: (0, jnp.minimum(j, first - 1))
    far = lambda j: (0, jnp.maximum(j - first, 0))
    return pl.pallas_call(
        functools.partial(heads_body, counts, len(groups[0])),
        grid=(first + last,),
        in_specs=[pl.BlockSpec((WIDTH, TILE), lambda j: (0, j))]
        + row_specs(groups[0], near)
        + row_specs(groups[1], far)
        + hbm(len(after)),
        out_specs=pl.BlockSpec((WIDTH, SEQ), lambda j: (0, 0)),
        scratch_shapes=[pltpu.VMEM((WIDTH, SEQ), F32)],
        out_shape=jax.ShapeDtypeStruct((WIDTH, SEQ), BF16),
        compiler_params=params(),
        cost_estimate=cost(2 * WIDTH * SEQ * D, 2 * (WIDTH * SEQ + SEQ * D + WIDTH * D)),
        name="heads_grad",
    )(weights, *groups[0], *groups[1], *after)


def rank(x, c):
    return (x % XS) * CS + c


ONWARD = [(rank(x, c), rank(x + 1 - 2 * c, c)) for x in range(XS) for c in range(CS)]
SIBLING = [(rank(x, c), rank(x, 1 - c)) for x in range(XS) for c in range(CS)]


def send(value, perm):
    return lax.ppermute(value, ("x", "c"), perm)


def hold_body(*refs):
    pass


def hold(value, *after):
    return pl.pallas_call(
        hold_body,
        in_specs=hbm(1 + len(after)),
        out_specs=hbm(1)[0],
        out_shape=jax.ShapeDtypeStruct(value.shape, value.dtype),
        input_output_aliases={0: 0},
        compiler_params=params(),
        cost_estimate=cost(0, 0),
        name="hold",
    )(value, *after)


def pair_body(own_ref, sib_ref, *refs):
    out_ref = refs[-1]
    out_ref[:TOK] = own_ref[...]
    out_ref[TOK:] = sib_ref[...]


def pair_up(own, sib, start, wide, after):
    at = start // TILE
    spec = pl.BlockSpec((TOK, TILE), lambda j: (0, j + at))
    return pl.pallas_call(
        pair_body,
        grid=(wide // TILE,),
        in_specs=[spec] * 2 + hbm(len(after)),
        out_specs=pl.BlockSpec((2 * TOK, TILE), lambda j: (0, j)),
        out_shape=jax.ShapeDtypeStruct((2 * TOK, wide), BF16),
        compiler_params=params(),
        cost_estimate=cost(0, 8 * TOK * wide),
        name="pair_up",
    )(own, sib, *after)


def slot_table():
    x, c = lax.axis_index("x"), lax.axis_index("c")
    step = 1 - 2 * c
    at = lambda xx, cc: lax.rem(xx + 2 * XS, XS) * CS + cc
    return jnp.stack(
        [
            at(x, c),
            at(x, 1 - c),
            at(x - step, c),
            at(x - step, 1 - c),
            at(x + step, 1 - c),
            at(x + step, c),
            at(x + 2, c),
            at(x + 2, 1 - c),
        ]
    ).astype(jnp.int32)


def exchange(value, axis):
    return lax.all_to_all(value, axis, split_axis=0, concat_axis=0, tiled=True)


def clip_order(seen):
    y, z = seen * lax.axis_index("y"), lax.axis_index("z")
    return jnp.stack([(y + i) % YS * ZS + (z + j) % ZS for i in range(YS) for j in range(ZS)]).astype(jnp.int32)


def around(parts, axis, size):
    return [parts[0]] + [
        lax.ppermute(parts[i], axis, [(a, (a + i) % size) for a in range(size)]) for i in range(1, size)
    ]


def total(parts):
    return functools.reduce(jnp.add, [p.astype(F32) for p in parts])


def scatter_sum(part):
    part = part.astype(BF16)
    return total(around([part[i * ROW : (i + 1) * ROW] for i in range(ZS)], "z", ZS))


def local(queries, keys, values, cotangent, gate, w_out):
    slots = slot_table()
    cot = cotangent[0, 0]
    to_context = lambda value: lax.ppermute(value, "b", [(0, 1)])

    other = to_context(cot)
    packed = pack(queries[0, 0], keys[0, 0], values[0, 0])
    qkv = exchange(packed, ("x", "c"))
    own = gated(gate[0], cot, other, 0, D, after=[packed])
    sib = send(own, SIBLING)
    weights = lax.all_gather(hold(w_out[0], sib, qkv), ("y", "z"), axis=0, tiled=True)
    pair0 = pair_up(own, sib, STARTS[0], CHUNKS[0], [])
    near0 = send(pair0, ONWARD)
    prob, att = forward(slots, qkv, after=[pair0])
    pair1 = pair_up(own, sib, STARTS[1], CHUNKS[1], [att, near0])
    near1 = send(pair1, ONWARD)
    near0 = hold(near0, pair1)
    far0 = hold(send(near0[:TOK], ONWARD), near1)
    pieces0 = [pair0, near0, send(near0, SIBLING), far0, send(far0, SIBLING)]
    (first_term,) = weight_grad(clip_order(0), att, pieces0, False)
    far1 = send(near1[:TOK], ONWARD)
    far1 = hold(far1, first_term)
    pieces1 = [pair1, near1, send(near1, SIBLING), far1, send(far1, SIBLING)]
    last_term = weight_grad(clip_order(1), att, pieces1, True)
    gt = heads_grad(weights, (pieces0, pieces1), after=last_term[:1])
    home = backward(slots, qkv, prob, gt, att)
    got = hold(exchange(first_term, "y"), home)
    last = around(last_term, "y", YS)
    last[0] = hold(last[0], got)
    first_sum = scatter_sum(jnp.sum(got.astype(F32), axis=0))
    last_sum = scatter_sum(total(last))
    dq, dk, dv = unpack(exchange(home, ("x", "c")))
    return (
        dq[None, None],
        dk[None, None],
        dv[None, None],
        jnp.concatenate([first_sum, last_sum], axis=1)[None],
    )


def solution(mesh):
    fine = Mesh(mesh.devices.reshape(2, XS, CS, YS, ZS), ("b", "x", "c", "y", "z"))
    tokens = P("b", ("y", "z"), ("x", "c"), None)
    weight = P("b", ("x", "c", "y", "z"), None)
    return jax.shard_map(
        local,
        mesh=fine,
        in_specs=(tokens, tokens, tokens, tokens, P("b", ("y", "z"), None), weight),
        out_specs=(tokens, tokens, tokens, weight),
        check_vma=False,
    )
```

```python
import functools

import jax
import jax.numpy as jnp
from jax import lax
from jax.experimental import pallas as pl
from jax.experimental.pallas import tpu as pltpu
from jax.sharding import Mesh, PartitionSpec as P

HD = 128
XS, CS, YS, ZS = 4, 2, 4, 4
RANKS = XS * CS
TOK = 128
SEQ = RANKS * TOK
NH = 3
WIDTH = NH * HD
D = 5120
TILE = 1024
GATE_TILE = 2560
SCALE = HD**-0.5
LOG2E = 1.4426950408889634
F32 = jnp.float32
BF16 = jnp.bfloat16
NT = (((1,), (1,)), ((), ()))
NN = (((1,), (0,)), ((), ()))
CHUNKS = (2048, 3072)
STARTS = tuple(sum(CHUNKS[:i]) for i in range(len(CHUNKS)))
ROW = WIDTH // (YS * ZS)
BLOCK = WIDTH // YS
VMEM_LIMIT = 56 * 1024 * 1024


def dot(a, b, dims=NN):
    return lax.dot_general(a, b, dims, preferred_element_type=F32)


def params(**more):
    return pltpu.CompilerParams(vmem_limit_bytes=VMEM_LIMIT, **more)


def cost(flops, nbytes, trans=0):
    return pl.CostEstimate(flops=flops, bytes_accessed=nbytes, transcendentals=trans)


def hbm(count):
    return [pl.BlockSpec(memory_space=pl.ANY)] * count


def pack_body(q_ref, k_ref, v_ref, out_ref):
    for r in range(RANKS):
        for i, ref in enumerate((q_ref, k_ref, v_ref)):
            out_ref[r, i] = ref[:, r * WIDTH : (r + 1) * WIDTH]


def pack(q, k, v):
    whole = pl.BlockSpec((TOK, RANKS * WIDTH), lambda j: (0, 0))
    return pl.pallas_call(
        pack_body,
        grid=(1,),
        in_specs=[whole] * 3,
        out_specs=pl.BlockSpec((RANKS, 3, TOK, WIDTH), lambda j: (0, 0, 0, 0)),
        out_shape=jax.ShapeDtypeStruct((RANKS, 3, TOK, WIDTH), BF16),
        compiler_params=params(),
        cost_estimate=cost(0, 2 * 3 * 2 * SEQ * WIDTH),
        name="pack",
    )(q, k, v)


def unpack_body(home_ref, *outs):
    for r in range(RANKS):
        for i, out in enumerate(outs):
            out[:, r * WIDTH : (r + 1) * WIDTH] = home_ref[r, i]


def unpack(home):
    whole = pl.BlockSpec((TOK, RANKS * WIDTH), lambda j: (0, 0))
    return pl.pallas_call(
        unpack_body,
        grid=(1,),
        in_specs=[pl.BlockSpec(home.shape, lambda j: (0, 0, 0, 0))],
        out_specs=[whole] * 3,
        out_shape=[jax.ShapeDtypeStruct((TOK, RANKS * WIDTH), BF16)] * 3,
        compiler_params=params(),
        cost_estimate=cost(0, 2 * 3 * 2 * SEQ * WIDTH),
        name="unpack",
    )(home)


def gate_body(gate_ref, mine_ref, other_ref, *refs):
    out_ref = refs[-1]
    total = mine_ref[...].astype(F32) + other_ref[...].astype(F32)
    out_ref[...] = (gate_ref[...] * total).astype(BF16)


def gated(gate, cot, other, start, wide, after=()):
    at = start // GATE_TILE
    return pl.pallas_call(
        gate_body,
        grid=(wide // GATE_TILE,),
        in_specs=[
            pl.BlockSpec((1, GATE_TILE), lambda j: (0, j + at)),
            pl.BlockSpec((TOK, GATE_TILE), lambda j: (0, j + at)),
            pl.BlockSpec((TOK, GATE_TILE), lambda j: (0, j + at)),
        ]
        + hbm(len(after)),
        out_specs=pl.BlockSpec((TOK, GATE_TILE), lambda j: (0, j)),
        out_shape=jax.ShapeDtypeStruct((TOK, wide), BF16),
        compiler_params=params(),
        cost_estimate=cost(2 * TOK * wide, 6 * TOK * wide),
        name="gated",
    )(gate, cot, other, *after)


def forward_body(slot_ref, qkv_ref, *refs):
    prob_ref, att_ref, q_s, k_s, vt_s = refs[-5:]
    for s in range(RANKS):
        rows = pl.ds(s * TOK, TOK)
        piece = slot_ref[s]
        q_s[rows, :] = qkv_ref[piece, 0]
        k_s[rows, :] = qkv_ref[piece, 1]
        vt_s[:, rows] = qkv_ref[piece, 2].astype(F32).T.astype(BF16)
    scores = dot(k_s[...], q_s[...], NT)
    top = jnp.max(scores, axis=0, keepdims=True)
    e = jnp.exp2((scores - top) * (SCALE * LOG2E))
    norm = 1.0 / jnp.sum(e, axis=0, keepdims=True)
    prob = (e * norm).astype(BF16)
    prob_ref[0] = prob
    att_ref[...] = dot(vt_s[...], prob).astype(BF16)


def forward(slots, qkv, after=()):
    return pl.pallas_call(
        forward_body,
        grid_spec=pltpu.PrefetchScalarGridSpec(
            num_scalar_prefetch=1,
            grid=(NH,),
            in_specs=[pl.BlockSpec((RANKS, 3, TOK, HD), lambda h, s: (0, 0, 0, h))] + hbm(len(after)),
            out_specs=[
                pl.BlockSpec((1, SEQ, SEQ), lambda h, s: (h, 0, 0)),
                pl.BlockSpec((HD, SEQ), lambda h, s: (h, 0)),
            ],
            scratch_shapes=[
                pltpu.VMEM((SEQ, HD), BF16),
                pltpu.VMEM((SEQ, HD), BF16),
                pltpu.VMEM((HD, SEQ), BF16),
            ],
        ),
        out_shape=[
            jax.ShapeDtypeStruct((NH, SEQ, SEQ), BF16),
            jax.ShapeDtypeStruct((WIDTH, SEQ), BF16),
        ],
        compiler_params=params(),
        cost_estimate=cost(4 * NH * SEQ * SEQ * HD, 2 * NH * SEQ * SEQ + 8 * SEQ * WIDTH, NH * SEQ * SEQ),
        name="forward",
    )(slots, qkv, *after)


def row_specs(pieces, index):
    return [pl.BlockSpec((p.shape[0], TILE), index) for p in pieces]


def weight_body(base, parts, count, at_ref, att_ref, *refs):
    outs, wide_s, att_s = refs[parts + count : -2], refs[-2], refs[-1]
    row = ROW

    @pl.when(pl.program_id(0) == 0)
    def _():
        wide_s[...] = att_ref[...].astype(F32)
        for i in range(YS * ZS):
            start = pl.multiple_of(at_ref[base + i] * row, 8)
            att_s[pl.ds(i * row, row), :] = wide_s[pl.ds(start, row), :]

    rows = jnp.concatenate([ref[...] for ref in refs[:parts]], axis=0)
    term = dot(att_s[...].astype(BF16), rows).astype(BF16)
    for i in range(YS):
        block = term[i * BLOCK : (i + 1) * BLOCK]
        if len(outs) == 1:
            outs[0][i] = block
        else:
            outs[i][...] = block


def weight_grad(table, base, att, pieces, split, after=()):
    wide = pieces[0].shape[1]
    return pl.pallas_call(
        functools.partial(weight_body, base, len(pieces), len(after)),
        grid_spec=pltpu.PrefetchScalarGridSpec(
            num_scalar_prefetch=1,
            grid=(wide // TILE,),
            in_specs=[pl.BlockSpec((WIDTH, SEQ), lambda j, o: (0, 0))] + row_specs(pieces, lambda j, o: (0, j)) + hbm(len(after)),
            out_specs=[pl.BlockSpec((BLOCK, TILE), lambda j, o: (0, j))] * YS
            if split
            else [pl.BlockSpec((YS, BLOCK, TILE), lambda j, o: (0, 0, j))],
            scratch_shapes=[pltpu.VMEM((WIDTH, SEQ), F32), pltpu.VMEM((WIDTH, SEQ), F32)],
        ),
        out_shape=[jax.ShapeDtypeStruct((BLOCK, wide), BF16)] * YS
        if split
        else [jax.ShapeDtypeStruct((YS, BLOCK, wide), BF16)],
        compiler_params=params(),
        cost_estimate=cost(2 * WIDTH * SEQ * wide, 2 * (WIDTH * SEQ + SEQ * wide + WIDTH * wide)),
        name="weight_grad",
    )(table, att, *pieces, *after)


def backward_body(counts, parts, slot_ref, w_ref, *refs):
    qkv_ref, prob_ref, att_ref = refs[2 * parts : 2 * parts + 3]
    out_ref, acc_s, gt_s, q_s, v_s, kt_s = refs[-6:]
    step = pl.program_id(0)

    @pl.when(step == 0)
    def _():
        acc_s[...] = jnp.zeros_like(acc_s)

    begin = 0
    for i, count in enumerate(counts):
        pieces = refs[i * parts : (i + 1) * parts]

        @pl.when((step >= begin) & (step < begin + count))
        def _():
            rows = jnp.concatenate([ref[...] for ref in pieces], axis=0)
            acc_s[...] += dot(w_ref[...], rows, NT)

        begin += count

    @pl.when(step == begin - 1)
    def _():
        for h in range(NH):
            gt_s[h] = acc_s[h * HD : (h + 1) * HD, :].astype(BF16)

    @pl.when(step >= begin)
    def _():
        for s in range(RANKS):
            rows = pl.ds(s * TOK, TOK)
            piece = slot_ref[s]
            q_s[rows, :] = qkv_ref[piece, 0]
            kt_s[:, rows] = qkv_ref[piece, 1].astype(F32).T.astype(BF16)
            v_s[rows, :] = qkv_ref[piece, 2]
        gt = gt_s[step - begin]
        prob = prob_ref[0]
        delta = jnp.sum(gt.astype(F32) * att_ref[...].astype(F32), axis=0, keepdims=True)
        dprob = dot(v_s[...], gt)
        dscore = (prob.astype(F32) * (dprob - delta)).astype(BF16)
        grads = (
            (dot(kt_s[...], dscore) * SCALE).T.astype(BF16),
            (dot(dscore, q_s[...]) * SCALE).astype(BF16),
            dot(prob, gt, NT).astype(BF16),
        )
        for s in range(RANKS):
            for i, grad in enumerate(grads):
                out_ref[slot_ref[s], i] = grad[s * TOK : (s + 1) * TOK]


def backward(slots, weights, groups, qkv, prob, att, after=()):
    counts = [g[0].shape[1] // TILE for g in groups]
    first, last = counts
    both = first + last
    near = lambda j, s: (0, jnp.minimum(j, first - 1))
    far = lambda j, s: (0, jnp.clip(j - first, 0, last - 1))
    head = lambda j: jnp.maximum(j - both, 0)
    return pl.pallas_call(
        functools.partial(backward_body, counts, len(groups[0])),
        grid_spec=pltpu.PrefetchScalarGridSpec(
            num_scalar_prefetch=1,
            grid=(both + NH,),
            in_specs=[pl.BlockSpec((WIDTH, TILE), lambda j, s: (0, jnp.minimum(j, both - 1)))]
            + row_specs(groups[0], near)
            + row_specs(groups[1], far)
            + [
                pl.BlockSpec((RANKS, 3, TOK, HD), lambda j, s: (0, 0, 0, head(j))),
                pl.BlockSpec((1, SEQ, SEQ), lambda j, s: (head(j), 0, 0)),
                pl.BlockSpec((HD, SEQ), lambda j, s: (head(j), 0)),
            ]
            + hbm(len(after)),
            out_specs=pl.BlockSpec((RANKS, 3, TOK, HD), lambda j, s: (0, 0, 0, head(j))),
            scratch_shapes=[
                pltpu.VMEM((WIDTH, SEQ), F32),
                pltpu.VMEM((NH, HD, SEQ), BF16),
                pltpu.VMEM((SEQ, HD), BF16),
                pltpu.VMEM((SEQ, HD), BF16),
                pltpu.VMEM((HD, SEQ), BF16),
            ],
        ),
        out_shape=jax.ShapeDtypeStruct((RANKS, 3, TOK, WIDTH), BF16),
        compiler_params=params(),
        cost_estimate=cost(2 * WIDTH * SEQ * D + 8 * NH * SEQ * SEQ * HD, 2 * (SEQ * D + WIDTH * D + NH * SEQ * SEQ + 8 * SEQ * WIDTH)),
        name="backward",
    )(slots, weights, *groups[0], *groups[1], qkv, prob, att, *after)


def rank(x, c):
    return (x % XS) * CS + c


ONWARD = [(rank(x, c), rank(x + 1 - 2 * c, c)) for x in range(XS) for c in range(CS)]
SIBLING = [(rank(x, c), rank(x, 1 - c)) for x in range(XS) for c in range(CS)]


def send(value, perm):
    return lax.ppermute(value, ("x", "c"), perm)


def hold_body(*refs):
    pass


def hold(value, *after):
    return pl.pallas_call(
        hold_body,
        in_specs=hbm(1 + len(after)),
        out_specs=hbm(1)[0],
        out_shape=jax.ShapeDtypeStruct(value.shape, value.dtype),
        input_output_aliases={0: 0},
        compiler_params=params(),
        cost_estimate=cost(0, 0),
        name="hold",
    )(value, *after)


def pair_body(own_ref, sib_ref, *refs):
    out_ref = refs[-1]
    out_ref[:TOK] = own_ref[...]
    out_ref[TOK:] = sib_ref[...]


def pair_up(own, sib, start, wide, after):
    at = start // TILE
    spec = pl.BlockSpec((TOK, TILE), lambda j: (0, j + at))
    return pl.pallas_call(
        pair_body,
        grid=(wide // TILE,),
        in_specs=[spec] * 2 + hbm(len(after)),
        out_specs=pl.BlockSpec((2 * TOK, TILE), lambda j: (0, j)),
        out_shape=jax.ShapeDtypeStruct((2 * TOK, wide), BF16),
        compiler_params=params(),
        cost_estimate=cost(0, 8 * TOK * wide),
        name="pair_up",
    )(own, sib, *after)


def slot_table():
    x, c = lax.axis_index("x"), lax.axis_index("c")
    step = 1 - 2 * c
    at = lambda xx, cc: lax.rem(xx + 2 * XS, XS) * CS + cc
    return (
        [
            at(x, c),
            at(x, 1 - c),
            at(x - step, c),
            at(x - step, 1 - c),
            at(x + step, 1 - c),
            at(x + step, c),
            at(x + 2, c),
            at(x + 2, 1 - c),
        ]
    )


def exchange(value, axis):
    return lax.all_to_all(value, axis, split_axis=0, concat_axis=0, tiled=True)


def clip_order(seen):
    y, z = seen * lax.axis_index("y"), lax.axis_index("z")
    return [(y + i) % YS * ZS + (z + j) % ZS for i in range(YS) for j in range(ZS)]


def around(parts, axis, size):
    return [parts[0]] + [
        lax.ppermute(parts[i], axis, [(a, (a + i) % size) for a in range(size)]) for i in range(1, size)
    ]


def total(parts):
    return functools.reduce(jnp.add, [p.astype(F32) for p in parts])


def scatter_sum(part):
    part = part.astype(BF16)
    return total(around([part[i * ROW : (i + 1) * ROW] for i in range(ZS)], "z", ZS))


def local(queries, keys, values, cotangent, gate, w_out):
    table = jnp.stack(slot_table() + clip_order(0) + clip_order(1)).astype(jnp.int32)
    cot = cotangent[0, 0]
    to_context = lambda value: lax.ppermute(value, "b", [(0, 1)])

    other = to_context(cot)
    packed = pack(queries[0, 0], keys[0, 0], values[0, 0])
    qkv = exchange(packed, ("x", "c"))
    own = gated(gate[0], cot, other, 0, D, after=[packed])
    sib = send(own, SIBLING)
    weights = lax.all_gather(hold(w_out[0], sib, qkv), ("y", "z"), axis=0, tiled=True)
    pair0 = pair_up(own, sib, STARTS[0], CHUNKS[0], [])
    near0 = send(pair0, ONWARD)
    prob, att = forward(table, qkv, after=[pair0])
    pair1 = hold(pair_up(own, sib, STARTS[1], CHUNKS[1], []), near0, att)
    near1 = send(pair1, ONWARD)
    near0 = hold(near0, pair1)
    far0 = hold(send(near0[:TOK], ONWARD), near1)
    pieces0 = [pair0, near0, send(near0, SIBLING), far0, send(far0, SIBLING)]
    (first_term,) = weight_grad(table, RANKS, att, pieces0, False)
    far1 = send(near1[:TOK], ONWARD)
    far1 = hold(far1, first_term)
    pieces1 = [pair1, near1, send(near1, SIBLING), far1, send(far1, SIBLING)]
    last_term = weight_grad(table, RANKS + YS * ZS, att, pieces1, True)
    home = backward(table, weights, (pieces0, pieces1), qkv, prob, att, after=last_term[:1])
    got = hold(exchange(first_term, "y"), home)
    last = around(last_term, "y", YS)
    last[0] = hold(last[0], got)
    first_sum = scatter_sum(jnp.sum(got.astype(F32), axis=0))
    last_sum = scatter_sum(total(last))
    dq, dk, dv = unpack(exchange(home, ("x", "c")))
    return (
        dq[None, None],
        dk[None, None],
        dv[None, None],
        jnp.concatenate([first_sum, last_sum], axis=1)[None],
    )


def solution(mesh):
    fine = Mesh(mesh.devices.reshape(2, XS, CS, YS, ZS), ("b", "x", "c", "y", "z"))
    tokens = P("b", ("y", "z"), ("x", "c"), None)
    weight = P("b", ("x", "c", "y", "z"), None)
    return jax.shard_map(
        local,
        mesh=fine,
        in_specs=(tokens, tokens, tokens, tokens, P("b", ("y", "z"), None), weight),
        out_specs=(tokens, tokens, tokens, weight),
        check_vma=False,
    )
```

```python
import functools

import jax
import jax.numpy as jnp
from jax import lax
from jax.experimental import pallas as pl
from jax.experimental.pallas import tpu as pltpu
from jax.sharding import Mesh, PartitionSpec as P

HD = 128
XS, CS, YS, ZS = 4, 2, 4, 4
RANKS = XS * CS
TOK = 128
SEQ = RANKS * TOK
NH = 3
WIDTH = NH * HD
D = 5120
TILE = 1024
GATE_TILE = 2560
SCALE = HD**-0.5
LOG2E = 1.4426950408889634
F32 = jnp.float32
BF16 = jnp.bfloat16
NT = (((1,), (1,)), ((), ()))
NN = (((1,), (0,)), ((), ()))
CHUNKS = (2048, 3072)
STARTS = tuple(sum(CHUNKS[:i]) for i in range(len(CHUNKS)))
ROW = WIDTH // (YS * ZS)
BLOCK = WIDTH // YS
VMEM_LIMIT = 56 * 1024 * 1024


def dot(a, b, dims=NN):
    return lax.dot_general(a, b, dims, preferred_element_type=F32)


def params(**more):
    return pltpu.CompilerParams(vmem_limit_bytes=VMEM_LIMIT, **more)


def cost(flops, nbytes, trans=0):
    return pl.CostEstimate(flops=flops, bytes_accessed=nbytes, transcendentals=trans)


def hbm(count):
    return [pl.BlockSpec(memory_space=pl.ANY)] * count


def pack_body(q_ref, k_ref, v_ref, out_ref):
    for r in range(RANKS):
        for i, ref in enumerate((q_ref, k_ref, v_ref)):
            out_ref[r, i] = ref[:, r * WIDTH : (r + 1) * WIDTH]


def pack(q, k, v):
    whole = pl.BlockSpec((TOK, RANKS * WIDTH), lambda j: (0, 0))
    return pl.pallas_call(
        pack_body,
        grid=(1,),
        in_specs=[whole] * 3,
        out_specs=pl.BlockSpec((RANKS, 3, TOK, WIDTH), lambda j: (0, 0, 0, 0)),
        out_shape=jax.ShapeDtypeStruct((RANKS, 3, TOK, WIDTH), BF16),
        compiler_params=params(),
        cost_estimate=cost(0, 2 * 3 * 2 * SEQ * WIDTH),
        name="pack",
    )(q, k, v)


def unpack_body(home_ref, *outs):
    for r in range(home_ref.shape[0]):
        for i, out in enumerate(outs):
            out[:, r * WIDTH : (r + 1) * WIDTH] = home_ref[r, i]


def unpack(home):
    half = RANKS // 2
    whole = pl.BlockSpec((TOK, half * WIDTH), lambda j: (0, j))
    return pl.pallas_call(
        unpack_body,
        grid=(2,),
        in_specs=[pl.BlockSpec((half, 3, TOK, WIDTH), lambda j: (j, 0, 0, 0))],
        out_specs=[whole] * 3,
        out_shape=[jax.ShapeDtypeStruct((TOK, RANKS * WIDTH), BF16)] * 3,
        compiler_params=params(),
        cost_estimate=cost(0, 2 * 3 * 2 * SEQ * WIDTH),
        name="unpack",
    )(home)


def gate_body(gate_ref, mine_ref, other_ref, *refs):
    out_ref = refs[-1]
    total = mine_ref[...].astype(F32) + other_ref[...].astype(F32)
    out_ref[...] = (gate_ref[...] * total).astype(BF16)


def gated(gate, cot, other, start, wide, after=()):
    at = start // GATE_TILE
    return pl.pallas_call(
        gate_body,
        grid=(wide // GATE_TILE,),
        in_specs=[
            pl.BlockSpec((1, GATE_TILE), lambda j: (0, j + at)),
            pl.BlockSpec((TOK, GATE_TILE), lambda j: (0, j + at)),
            pl.BlockSpec((TOK, GATE_TILE), lambda j: (0, j + at)),
        ]
        + hbm(len(after)),
        out_specs=pl.BlockSpec((TOK, GATE_TILE), lambda j: (0, j)),
        out_shape=jax.ShapeDtypeStruct((TOK, wide), BF16),
        compiler_params=params(),
        cost_estimate=cost(2 * TOK * wide, 6 * TOK * wide),
        name="gated",
    )(gate, cot, other, *after)


def forward_body(slot_ref, qkv_ref, *refs):
    prob_ref, att_ref, q_s, k_s, vt_s = refs[-5:]
    for s in range(RANKS):
        rows = pl.ds(s * TOK, TOK)
        piece = slot_ref[s]
        q_s[rows, :] = qkv_ref[piece, 0]
        k_s[rows, :] = qkv_ref[piece, 1]
        vt_s[:, rows] = qkv_ref[piece, 2].astype(F32).T.astype(BF16)
    scores = dot(k_s[...], q_s[...], NT)
    top = jnp.max(scores, axis=0, keepdims=True)
    e = jnp.exp2((scores - top) * (SCALE * LOG2E))
    norm = 1.0 / jnp.sum(e, axis=0, keepdims=True)
    prob = (e * norm).astype(BF16)
    prob_ref[0] = prob
    att_ref[...] = dot(vt_s[...], prob).astype(BF16)


def forward(slots, qkv, after=()):
    return pl.pallas_call(
        forward_body,
        grid_spec=pltpu.PrefetchScalarGridSpec(
            num_scalar_prefetch=1,
            grid=(NH,),
            in_specs=[pl.BlockSpec((RANKS, 3, TOK, HD), lambda h, s: (0, 0, 0, h))] + hbm(len(after)),
            out_specs=[
                pl.BlockSpec((1, SEQ, SEQ), lambda h, s: (h, 0, 0)),
                pl.BlockSpec((HD, SEQ), lambda h, s: (h, 0)),
            ],
            scratch_shapes=[
                pltpu.VMEM((SEQ, HD), BF16),
                pltpu.VMEM((SEQ, HD), BF16),
                pltpu.VMEM((HD, SEQ), BF16),
            ],
        ),
        out_shape=[
            jax.ShapeDtypeStruct((NH, SEQ, SEQ), BF16),
            jax.ShapeDtypeStruct((WIDTH, SEQ), BF16),
        ],
        compiler_params=params(),
        cost_estimate=cost(4 * NH * SEQ * SEQ * HD, 2 * NH * SEQ * SEQ + 8 * SEQ * WIDTH, NH * SEQ * SEQ),
        name="forward",
    )(slots, qkv, *after)


def row_specs(pieces, index):
    return [pl.BlockSpec((p.shape[0], TILE), index) for p in pieces]


def weight_body(base, parts, count, at_ref, att_ref, *refs):
    outs, wide_s, att_s = refs[parts + count : -2], refs[-2], refs[-1]
    row = ROW

    @pl.when(pl.program_id(0) == 0)
    def _():
        wide_s[...] = att_ref[...].astype(F32)
        for i in range(YS * ZS):
            start = pl.multiple_of(at_ref[base + i] * row, 8)
            att_s[pl.ds(i * row, row), :] = wide_s[pl.ds(start, row), :]

    rows = jnp.concatenate([ref[...] for ref in refs[:parts]], axis=0)
    term = dot(att_s[...].astype(BF16), rows).astype(BF16)
    for i in range(YS):
        block = term[i * BLOCK : (i + 1) * BLOCK]
        if len(outs) == 1:
            outs[0][i] = block
        else:
            outs[i][...] = block


def weight_grad(table, base, att, pieces, split, after=()):
    wide = pieces[0].shape[1]
    return pl.pallas_call(
        functools.partial(weight_body, base, len(pieces), len(after)),
        grid_spec=pltpu.PrefetchScalarGridSpec(
            num_scalar_prefetch=1,
            grid=(wide // TILE,),
            in_specs=[pl.BlockSpec((WIDTH, SEQ), lambda j, o: (0, 0))] + row_specs(pieces, lambda j, o: (0, j)) + hbm(len(after)),
            out_specs=[pl.BlockSpec((BLOCK, TILE), lambda j, o: (0, j))] * YS
            if split
            else [pl.BlockSpec((YS, BLOCK, TILE), lambda j, o: (0, 0, j))],
            scratch_shapes=[pltpu.VMEM((WIDTH, SEQ), F32), pltpu.VMEM((WIDTH, SEQ), F32)],
        ),
        out_shape=[jax.ShapeDtypeStruct((BLOCK, wide), BF16)] * YS
        if split
        else [jax.ShapeDtypeStruct((YS, BLOCK, wide), BF16)],
        compiler_params=params(),
        cost_estimate=cost(2 * WIDTH * SEQ * wide, 2 * (WIDTH * SEQ + SEQ * wide + WIDTH * wide)),
        name="weight_grad",
    )(table, att, *pieces, *after)


def backward_body(counts, parts, slot_ref, w_ref, *refs):
    qkv_ref, prob_ref, att_ref = refs[2 * parts : 2 * parts + 3]
    out_ref, acc_s, gt_s, q_s, v_s, kt_s = refs[-6:]
    step = pl.program_id(0)

    @pl.when(step == 0)
    def _():
        acc_s[...] = jnp.zeros_like(acc_s)

    begin = 0
    for i, count in enumerate(counts):
        pieces = refs[i * parts : (i + 1) * parts]

        @pl.when((step >= begin) & (step < begin + count))
        def _():
            rows = jnp.concatenate([ref[...] for ref in pieces], axis=0)
            acc_s[...] += dot(w_ref[...], rows, NT)

        begin += count

    @pl.when(step == begin - 1)
    def _():
        for h in range(NH):
            gt_s[h] = acc_s[h * HD : (h + 1) * HD, :].astype(BF16)

    @pl.when(step >= begin)
    def _():
        for s in range(RANKS):
            rows = pl.ds(s * TOK, TOK)
            piece = slot_ref[s]
            q_s[rows, :] = qkv_ref[piece, 0]
            kt_s[:, rows] = qkv_ref[piece, 1].astype(F32).T.astype(BF16)
            v_s[rows, :] = qkv_ref[piece, 2]
        gt = gt_s[step - begin]
        prob = prob_ref[0]
        delta = jnp.sum(gt.astype(F32) * att_ref[...].astype(F32), axis=0, keepdims=True)
        dprob = dot(v_s[...], gt)
        dscore = (prob.astype(F32) * (dprob - delta)).astype(BF16)
        grads = (
            (dot(kt_s[...], dscore) * SCALE).T.astype(BF16),
            (dot(dscore, q_s[...]) * SCALE).astype(BF16),
            dot(prob, gt, NT).astype(BF16),
        )
        for s in range(RANKS):
            for i, grad in enumerate(grads):
                out_ref[slot_ref[s], i] = grad[s * TOK : (s + 1) * TOK]


def backward(slots, weights, groups, qkv, prob, att, after=()):
    counts = [g[0].shape[1] // TILE for g in groups]
    first, last = counts
    both = first + last
    near = lambda j, s: (0, jnp.minimum(j, first - 1))
    far = lambda j, s: (0, jnp.clip(j - first, 0, last - 1))
    head = lambda j: jnp.maximum(j - both, 0)
    return pl.pallas_call(
        functools.partial(backward_body, counts, len(groups[0])),
        grid_spec=pltpu.PrefetchScalarGridSpec(
            num_scalar_prefetch=1,
            grid=(both + NH,),
            in_specs=[pl.BlockSpec((WIDTH, TILE), lambda j, s: (0, jnp.minimum(j, both - 1)))]
            + row_specs(groups[0], near)
            + row_specs(groups[1], far)
            + [
                pl.BlockSpec((RANKS, 3, TOK, HD), lambda j, s: (0, 0, 0, head(j))),
                pl.BlockSpec((1, SEQ, SEQ), lambda j, s: (head(j), 0, 0)),
                pl.BlockSpec((HD, SEQ), lambda j, s: (head(j), 0)),
            ]
            + hbm(len(after)),
            out_specs=pl.BlockSpec((RANKS, 3, TOK, HD), lambda j, s: (0, 0, 0, head(j))),
            scratch_shapes=[
                pltpu.VMEM((WIDTH, SEQ), F32),
                pltpu.VMEM((NH, HD, SEQ), BF16),
                pltpu.VMEM((SEQ, HD), BF16),
                pltpu.VMEM((SEQ, HD), BF16),
                pltpu.VMEM((HD, SEQ), BF16),
            ],
        ),
        out_shape=jax.ShapeDtypeStruct((RANKS, 3, TOK, WIDTH), BF16),
        compiler_params=params(),
        cost_estimate=cost(2 * WIDTH * SEQ * D + 8 * NH * SEQ * SEQ * HD, 2 * (SEQ * D + WIDTH * D + NH * SEQ * SEQ + 8 * SEQ * WIDTH)),
        name="backward",
    )(slots, weights, *groups[0], *groups[1], qkv, prob, att, *after)


def rank(x, c):
    return (x % XS) * CS + c


ONWARD = [(rank(x, c), rank(x + 1 - 2 * c, c)) for x in range(XS) for c in range(CS)]
SIBLING = [(rank(x, c), rank(x, 1 - c)) for x in range(XS) for c in range(CS)]


def send(value, perm):
    return lax.ppermute(value, ("x", "c"), perm)


def hold_body(*refs):
    pass


def hold(value, *after):
    return pl.pallas_call(
        hold_body,
        in_specs=hbm(1 + len(after)),
        out_specs=hbm(1)[0],
        out_shape=jax.ShapeDtypeStruct(value.shape, value.dtype),
        input_output_aliases={0: 0},
        compiler_params=params(),
        cost_estimate=cost(0, 0),
        name="hold",
    )(value, *after)


def pair_body(own_ref, sib_ref, *refs):
    out_ref = refs[-1]
    out_ref[:TOK] = own_ref[...]
    out_ref[TOK:] = sib_ref[...]


def pair_up(own, sib, start, wide, after):
    at = start // TILE
    spec = pl.BlockSpec((TOK, TILE), lambda j: (0, j + at))
    return pl.pallas_call(
        pair_body,
        grid=(wide // TILE,),
        in_specs=[spec] * 2 + hbm(len(after)),
        out_specs=pl.BlockSpec((2 * TOK, TILE), lambda j: (0, j)),
        out_shape=jax.ShapeDtypeStruct((2 * TOK, wide), BF16),
        compiler_params=params(),
        cost_estimate=cost(0, 8 * TOK * wide),
        name="pair_up",
    )(own, sib, *after)


def slot_table():
    x, c = lax.axis_index("x"), lax.axis_index("c")
    step = 1 - 2 * c
    at = lambda xx, cc: lax.rem(xx + 2 * XS, XS) * CS + cc
    return (
        [
            at(x, c),
            at(x, 1 - c),
            at(x - step, c),
            at(x - step, 1 - c),
            at(x + step, 1 - c),
            at(x + step, c),
            at(x + 2, c),
            at(x + 2, 1 - c),
        ]
    )


def exchange(value, axis):
    return lax.all_to_all(value, axis, split_axis=0, concat_axis=0, tiled=True)


def clip_order(seen):
    y, z = seen * lax.axis_index("y"), lax.axis_index("z")
    return [(y + i) % YS * ZS + (z + j) % ZS for i in range(YS) for j in range(ZS)]


def around(parts, axis, size):
    return [parts[0]] + [
        lax.ppermute(parts[i], axis, [(a, (a + i) % size) for a in range(size)]) for i in range(1, size)
    ]


def total(parts):
    return functools.reduce(jnp.add, [p.astype(F32) for p in parts])


def scatter_sum(part):
    part = part.astype(BF16)
    return total(around([part[i * ROW : (i + 1) * ROW] for i in range(ZS)], "z", ZS))


def local(queries, keys, values, cotangent, gate, w_out):
    table = jnp.stack(slot_table() + clip_order(0) + clip_order(1)).astype(jnp.int32)
    cot = cotangent[0, 0]
    to_context = lambda value: lax.ppermute(value, "b", [(0, 1)])

    other = to_context(cot)
    packed = pack(queries[0, 0], keys[0, 0], values[0, 0])
    qkv = exchange(packed, ("x", "c"))
    own = gated(gate[0], cot, other, 0, D, after=[packed])
    sib = send(own, SIBLING)
    weights = lax.all_gather(hold(w_out[0], sib, qkv), ("y", "z"), axis=0, tiled=True)
    pair0 = pair_up(own, sib, STARTS[0], CHUNKS[0], [])
    near0 = send(pair0, ONWARD)
    prob, att = forward(table, qkv, after=[pair0])
    pair1 = hold(pair_up(own, sib, STARTS[1], CHUNKS[1], []), near0, att)
    near1 = send(pair1, ONWARD)
    near0 = hold(near0, pair1)
    far0 = hold(send(near0[:TOK], ONWARD), near1)
    pieces0 = [pair0, near0, send(near0, SIBLING), far0, send(far0, SIBLING)]
    (first_term,) = weight_grad(table, RANKS, att, pieces0, False)
    far1 = send(near1[:TOK], ONWARD)
    far1 = hold(far1, first_term)
    pieces1 = [pair1, near1, send(near1, SIBLING), far1, send(far1, SIBLING)]
    last_term = weight_grad(table, RANKS + YS * ZS, att, pieces1, True)
    home = backward(table, weights, (pieces0, pieces1), qkv, prob, att, after=last_term[:1])
    got = hold(exchange(first_term, "y"), home)
    last = around(last_term, "y", YS)
    last[0] = hold(last[0], got)
    first_sum = scatter_sum(jnp.sum(got.astype(F32), axis=0))
    last_sum = scatter_sum(total(last))
    dq, dk, dv = unpack(exchange(home, ("x", "c")))
    return (
        dq[None, None],
        dk[None, None],
        dv[None, None],
        jnp.concatenate([first_sum, last_sum], axis=1)[None],
    )


def solution(mesh):
    fine = Mesh(mesh.devices.reshape(2, XS, CS, YS, ZS), ("b", "x", "c", "y", "z"))
    tokens = P("b", ("y", "z"), ("x", "c"), None)
    weight = P("b", ("x", "c", "y", "z"), None)
    return jax.shard_map(
        local,
        mesh=fine,
        in_specs=(tokens, tokens, tokens, tokens, P("b", ("y", "z"), None), weight),
        out_specs=(tokens, tokens, tokens, weight),
        check_vma=False,
    )
```
